32 devices in a mesh: freq: 2 (over y), col: 4 (over z), row: 2 (over x), help: 2 (over core).
Axes of the slice: x: 2, y: 2, z: 4, core: 2. Of those that a mesh axis runs over, the one named last changes fastest.
Arguments:
- wavefield: bfloat16 [4, 64, 512, 128], P('freq', 'col', ('row', 'help')), parts along dimension 0, may hold values from -6 to 6
- basis_factor: bfloat16 [4, 8, 64, 80, 512], P('freq', 'row', 'col', 'help'), parts along dimension 0, may hold values from -0.0625 to 0.0625
- second_factor: bfloat16 [4, 8, 64, 80, 512], P('freq', 'row', 'col', 'help'), parts along dimension 0, may hold values from -0.1875 to 0.1875
- tile_ranks: int32 [16, 64], P(('freq', 'row'), 'col'), parts along dimension 0, may hold values from 16 to 80
- observed: bfloat16 [4, 8, 512, 128], P('freq', 'row', ('col', 'help')), parts along dimension 0, may hold values from -6 to 6
- amplitude: bfloat16 [16, 512, 128], P(('freq', 'row'), ('col', 'help')), parts along dimension 0, may hold values from 0.29882812 to 3
Outputs:
- residual: bfloat16 [4, 8, 512, 128], P('freq', 'row', ('col', 'help')), parts along dimension 0
- adjoint: bfloat16 [4, 64, 512, 128], P('freq', 'col', ('row', 'help')), parts along dimension 0
The draws below stay inside these ranges and needn't reach their ends.
There are 2 independent parts, one for each index of `freq`. The reference program is written for one: setup_inputs(seed, part) draws one part's arguments, and reference() takes and returns one part's arrays. A program takes and returns all parts, laid end to end along the dimension named above; each array names one. Nothing has to cross between parts.
Inputs may be any that keep to these rules, and one draw needn't show every extreme that they name: `tile_ranks`: entries of a tile's factors at rank terms from its rank on are not part of the kernel.
All inputs are finite; a program needn't handle non-finite values.
Results may differ from the reference program's by a relative error of at most 0.006.
Values may be sent and summed in bfloat16 or wider, within the bound.
No kernel may reach another device: no remote copies, remote signals or barrier semaphores. Data moves between devices by JAX's collectives and lax.ppermute only.
A program may use at most 128 MiB of HBM per device.

```python
import math
import jax
import jax.numpy as jnp
from jax import lax

TILE = 512
RMAX = 80
RMIN = 16
RHS = 128
TC = 64
TR = 8


def plant(array, rng, low, high):
    dims = array.shape
    index_at = [jax.random.randint(jax.random.fold_in(rng, axis), (), 0, dims[axis]) for axis in range(len(dims))]
    array = array.at[tuple(index_at)].set(low)
    longest = dims.index(max(dims))
    index_at[longest] = (index_at[longest] + 1) % dims[longest]
    return array.at[tuple(index_at)].set(high)


def level_of(stream_key, extent, cuts, low, top_value):
    gain = 1.0
    for position, parts in cuts:
        draws = jax.random.uniform(jax.random.fold_in(jax.random.fold_in(stream_key, 6), position), (parts,), jnp.float32, low / len(cuts), top_value / len(cuts))
        gain = gain * jnp.repeat(jnp.exp(draws), extent[position] // parts).reshape((-1,) + (1,) * (len(extent) - 1 - position))
    return gain


def normal_values(rng, extent, scale, limit, split=(), kind=jnp.bfloat16):
    entries = scale * jax.random.normal(rng, extent, jnp.float32)
    if split:
        entries = entries * level_of(rng, extent, split, -0.22, 0.18)
    return jnp.clip(entries, -limit, limit).astype(kind)


def setup_inputs(seed: int = 0, part: int = 0) -> dict:
    splits = jax.random.split(jax.random.key(seed), 7)
    part_splits = jax.random.split(jax.random.fold_in(splits[6], part), 7)
    wavefield = normal_values(part_splits[0], (2, TC, TILE, RHS), 1.0, 6.0, ((1, 4), (2, 4)))
    basis_factor = normal_values(part_splits[1], (2, TR, TC, RMAX, TILE), (2 * TC * RMAX) ** -0.5, 0.0625, ((1, 2), (2, 4), (3, 2)))
    second_factor = normal_values(part_splits[2], (2, TR, TC, RMAX, TILE), (2 * TILE) ** -0.5, 0.1875, ((1, 2), (2, 4), (3, 2)))
    tile_ranks = plant(jax.random.randint(part_splits[3], (TR, TC), RMIN, RMAX + 1), jax.random.fold_in(part_splits[3], 1), RMIN, RMAX).astype(jnp.int32)
    observed = normal_values(part_splits[4], (2, TR, TILE, RHS), 1.0, 6.0, ((1, 2), (2, 8)))
    amplitude = jnp.clip(jnp.exp(math.log(3.0) - 2.306499 * jax.random.uniform(part_splits[5], (TR, TILE, RHS), jnp.float32) ** level_of(part_splits[5], (TR, TILE, RHS), ((0, 2), (1, 8)), -0.2, 0.2)), 0.29882812, 3.0).astype(jnp.bfloat16)
    return dict(wavefield=wavefield, basis_factor=basis_factor, second_factor=second_factor, tile_ranks=tile_ranks, observed=observed, amplitude=amplitude)


def settle(value):
    return lax.optimization_barrier(value.astype(jnp.bfloat16)).astype(jnp.float32)


def tile_row(basis_row, second_row, rank_row, waves, observed_row, amplitude_row):
    basis_row = basis_row.astype(jnp.float32)
    second_row = second_row.astype(jnp.float32)
    terms = jnp.arange(RMAX, dtype=jnp.int32)
    keep = (terms[None, :] < rank_row[:, None]).astype(jnp.float32)[:, :, None]
    coef_real = jnp.einsum('pjkt,pjtn->jkn', second_row, waves)
    coef_imag = jnp.einsum('jkt,jtn->jkn', second_row[0], waves[1]) - jnp.einsum('jkt,jtn->jkn', second_row[1], waves[0])
    coef_real = settle(coef_real * keep)
    coef_imag = settle(coef_imag * keep)
    forward_real = jnp.einsum('jks,jkn->sn', basis_row[0], coef_real) - jnp.einsum('jks,jkn->sn', basis_row[1], coef_imag)
    forward_imag = jnp.einsum('jks,jkn->sn', basis_row[0], coef_imag) + jnp.einsum('jks,jkn->sn', basis_row[1], coef_real)
    forward = jnp.stack([forward_real, forward_imag])
    weight = amplitude_row.astype(jnp.float32)[None]
    residual_row = (weight * (forward - observed_row.astype(jnp.float32))).astype(jnp.bfloat16)
    resid = residual_row.astype(jnp.float32)
    back_real = jnp.einsum('pjks,psn->jkn', basis_row, resid)
    back_imag = jnp.einsum('jks,sn->jkn', basis_row[0], resid[1]) - jnp.einsum('jks,sn->jkn', basis_row[1], resid[0])
    back_real = settle(back_real * keep)
    back_imag = settle(back_imag * keep)
    adjoint_real = jnp.einsum('jkt,jkn->jtn', second_row[0], back_real) - jnp.einsum('jkt,jkn->jtn', second_row[1], back_imag)
    adjoint_imag = jnp.einsum('jkt,jkn->jtn', second_row[0], back_imag) + jnp.einsum('jkt,jkn->jtn', second_row[1], back_real)
    return residual_row, jnp.stack([adjoint_real, adjoint_imag])


def reference(wavefield, basis_factor, second_factor, tile_ranks, observed, amplitude):
    waves = wavefield.astype(jnp.float32)

    def step(carry, index):
        basis_row = lax.dynamic_index_in_dim(basis_factor, index, 1, keepdims=False)
        second_row = lax.dynamic_index_in_dim(second_factor, index, 1, keepdims=False)
        rank_row = lax.dynamic_index_in_dim(tile_ranks, index, 0, keepdims=False)
        observed_row = lax.dynamic_index_in_dim(observed, index, 1, keepdims=False)
        amplitude_row = lax.dynamic_index_in_dim(amplitude, index, 0, keepdims=False)
        residual_row, term = tile_row(basis_row, second_row, rank_row, waves, observed_row, amplitude_row)
        return carry + term, residual_row

    start = jnp.zeros((2, TC, TILE, RHS), jnp.float32)
    total, residual_rows = lax.scan(step, start, jnp.arange(TR, dtype=jnp.int32))
    residual = jnp.moveaxis(residual_rows, 0, 1)
    return residual, total.astype(jnp.bfloat16)
```

```python
import functools

import jax
import jax.numpy as jnp
from jax import lax
from jax.experimental import pallas as pl
from jax.experimental.pallas import tpu as pltpu
from jax.sharding import PartitionSpec as P

BF16 = jnp.bfloat16
F32 = jnp.float32
CHUNKS = 2
STEP_TILES = 4


def swap(axis_name, step, value):
    size = lax.axis_size(axis_name)
    return lax.ppermute(value, axis_name, [(i, i ^ step) for i in range(size)])


def gather_pieces(value, axis_name):
    size = lax.axis_size(axis_name)
    return [value] + [swap(axis_name, step, value) for step in range(1, size)]


def turn(value, first, second):
    width = value.shape[-1]
    lane = lax.broadcasted_iota(jnp.int32, value.shape, value.ndim - 1)
    sign = jnp.where(lane < width // 2, first, second).astype(F32)
    return pltpu.roll(value, width // 2, value.ndim - 1) * sign


def forward_kernel(dims, scalars, *refs):
    tiles, rows, terms, rest, zs, helps, n_pieces, steps, peers = dims
    pieces = refs[:n_pieces]
    second, basis, keep_out, send_out, waves, coef, both = refs[n_pieces:]
    step = pl.program_id(0)
    here = scalars[0]
    quarter = pieces[0].shape[1]
    width = pieces[0].shape[2]

    @pl.when(step < steps)
    def _():
        row_index = lax.broadcasted_iota(jnp.int32, (terms, width), 0)
        for jj in range(tiles):
            for n, piece in enumerate(pieces):
                at = pl.multiple_of(scalars[1 + n] * quarter, quarter)
                waves[jj, pl.ds(at, quarter), :] = piece[jj]
            out = jnp.dot(second[jj], waves[jj], preferred_element_type=F32)
            half = rows * terms
            value = out[:half] + turn(out[half:], 1.0, -1.0)
            j = step * tiles + jj
            at = pl.multiple_of(j * terms, 8)
            for i in range(rows):
                left = scalars[rest + i * steps * tiles + j] - here * terms
                part = value[i * terms : (i + 1) * terms]
                coef[i, pl.ds(at, terms), :] = jnp.where(row_index < left, part, 0.0)

    @pl.when(step >= steps)
    def _():
        i = step - steps
        depth = coef.shape[1]
        value = coef[i]
        both[:depth, :] = value.astype(BF16)
        both[depth:, :] = turn(value, -1.0, 1.0).astype(BF16)
        span = keep_out.shape[2]
        for out_ref, h in ((keep_out, here), (send_out, 1 - here)):
            left = jnp.concatenate(
                [
                    basis[0, pl.ds(pl.multiple_of((scalars[peers + z] * helps + h) * span, span), span), :]
                    for z in range(zs)
                ],
                axis=0,
            )
            out = jnp.dot(left, both[...], preferred_element_type=F32)
            for z in range(zs):
                out_ref[z, 0] = out[z * span : (z + 1) * span].astype(out_ref.dtype)


def adjoint_kernel(dims, scalars, *refs):
    tiles, rows, terms, rest, rs, helps, n_pieces, steps, peers, places = dims
    pieces = refs[:n_pieces]
    basis, second, keep_out, send_out, resid, back, both = refs[n_pieces:]
    step = pl.program_id(0)
    here = scalars[0]
    span = pieces[0].shape[1]
    width = pieces[0].shape[2]
    columns = back.shape[0]

    @pl.when(step < rows)
    def _():
        for n, piece in enumerate(pieces):
            at = pl.multiple_of(scalars[places + n] * span, span)
            resid[pl.ds(at, span), :] = piece[0]
        value = resid[...]
        turned = turn(value.astype(F32), 1.0, -1.0).astype(BF16)
        out = jnp.dot(basis[0, 0], value, preferred_element_type=F32)
        out = out + jnp.dot(basis[1, 0], turned, preferred_element_type=F32)
        row_index = lax.broadcasted_iota(jnp.int32, (terms, width), 0)
        at = pl.multiple_of(step * terms, 8)
        for j in range(columns):
            left = scalars[rest + step * columns + j] - here * terms
            part = out[j * terms : (j + 1) * terms]
            back[j, pl.ds(at, terms), :] = jnp.where(row_index < left, part, 0.0)

    @pl.when(step >= rows)
    def _():
        depth = back.shape[1]
        quarter = keep_out.shape[2]
        for jj in range(tiles):
            value = back[(step - rows) * tiles + jj]
            both[jj, :depth, :] = value.astype(BF16)
            both[jj, depth:, :] = turn(value, -1.0, 1.0).astype(BF16)
            for out_ref, h in ((keep_out, here), (send_out, 1 - here)):
                left = jnp.concatenate(
                    [
                        second[
                            jj,
                            pl.ds(pl.multiple_of((scalars[peers + r] * helps + h) * quarter, quarter), quarter),
                            :,
                        ]
                        for r in range(rs)
                    ],
                    axis=0,
                )
                out = jnp.dot(left, both[jj], preferred_element_type=F32)
                for r in range(rs):
                    out_ref[r, jj] = out[r * quarter : (r + 1) * quarter].astype(out_ref.dtype)


def body(wavefield, basis_factor, second_factor, tile_ranks, observed, amplitude):
    _, columns, quarter, rhs = wavefield.shape
    _, rows, _, terms, tile = basis_factor.shape
    span = observed.shape[2]
    zs, rs, helps = lax.axis_size("col"), lax.axis_size("row"), lax.axis_size("help")
    z, r, h = lax.axis_index("col"), lax.axis_index("row"), lax.axis_index("help")
    part = rhs // CHUNKS
    width = 2 * part
    tiles = STEP_TILES
    steps = columns // tiles

    z_peers = [z ^ d for d in range(zs)]
    r_peers = [r ^ d for d in range(rs)]
    wave_places = [p * helps + (h ^ d) for d in range(helps) for p in r_peers]
    resid_places = [p * helps + (h ^ d) for d in range(helps) for p in z_peers]
    head = [h] + wave_places + z_peers + resid_places + r_peers
    z_at = 1 + len(wave_places)
    resid_at = z_at + zs
    r_at = resid_at + len(resid_places)
    rest = len(head)
    scalars = jnp.concatenate([jnp.stack(head).astype(jnp.int32), tile_ranks.reshape(-1)])

    def split(value, c):
        return jnp.concatenate(
            [value[0, ..., c * part : (c + 1) * part], value[1, ..., c * part : (c + 1) * part]], -1
        )

    second_rows = second_factor.transpose(2, 0, 1, 3, 4).reshape(columns, 2 * rows * terms, tile)
    second_cols = second_factor.transpose(2, 4, 0, 1, 3).reshape(columns, tile, 2 * rows * terms)
    basis_rows = basis_factor.reshape(2, rows, columns * terms, tile)
    basis_cols = basis_factor.transpose(1, 4, 0, 2, 3).reshape(rows, tile, 2 * columns * terms)

    def run_forward(pieces):
        n = len(pieces)
        dims = (tiles, rows, terms, rest, zs, helps, n, steps, z_at)
        out_block = pl.BlockSpec((zs, 1, span, width), lambda g, s: (0, jnp.maximum(g - steps, 0), 0, 0))
        return pl.pallas_call(
            functools.partial(forward_kernel, dims),
            out_shape=(
                jax.ShapeDtypeStruct((zs, rows, span, width), F32),
                jax.ShapeDtypeStruct((zs, rows, span, width), BF16),
            ),
            grid_spec=pltpu.PrefetchScalarGridSpec(
                num_scalar_prefetch=1,
                grid=(steps + rows,),
                in_specs=[
                    pl.BlockSpec((tiles, quarter, width), lambda g, s: (jnp.minimum(g, steps - 1), 0, 0))
                    for _ in range(n)
                ]
                + [
                    pl.BlockSpec(
                        (tiles, 2 * rows * terms, tile), lambda g, s: (jnp.minimum(g, steps - 1), 0, 0)
                    ),
                    pl.BlockSpec(
                        (1, tile, 2 * columns * terms), lambda g, s: (jnp.maximum(g - steps, 0), 0, 0)
                    ),
                ],
                out_specs=(out_block, out_block),
                scratch_shapes=[
                    pltpu.VMEM((tiles, tile, width), BF16),
                    pltpu.VMEM((rows, columns * terms, width), F32),
                    pltpu.VMEM((2 * columns * terms, width), BF16),
                ],
            ),
            compiler_params=pltpu.CompilerParams(vmem_limit_bytes=40 * 1024 * 1024),
            cost_estimate=pl.CostEstimate(
                flops=8 * 2 * rows * columns * terms * tile * width // 2,
                bytes_accessed=8 * rows * columns * terms * tile,
                transcendentals=0,
            ),
            name="forward_product",
        )(scalars, *pieces, second_rows, basis_cols)

    def run_adjoint(pieces):
        n = len(pieces)
        dims = (tiles, rows, terms, rest, rs, helps, n, rows, r_at, resid_at)
        out_block = pl.BlockSpec((rs, tiles, quarter, width), lambda g, s: (0, jnp.maximum(g - rows, 0), 0, 0))
        return pl.pallas_call(
            functools.partial(adjoint_kernel, dims),
            out_shape=(
                jax.ShapeDtypeStruct((rs, columns, quarter, width), F32),
                jax.ShapeDtypeStruct((rs, columns, quarter, width), BF16),
            ),
            grid_spec=pltpu.PrefetchScalarGridSpec(
                num_scalar_prefetch=1,
                grid=(rows + steps,),
                in_specs=[
                    pl.BlockSpec((1, span, width), lambda g, s: (jnp.minimum(g, rows - 1), 0, 0))
                    for _ in range(n)
                ]
                + [
                    pl.BlockSpec(
                        (2, 1, columns * terms, tile), lambda g, s: (0, jnp.minimum(g, rows - 1), 0, 0)
                    ),
                    pl.BlockSpec(
                        (tiles, tile, 2 * rows * terms), lambda g, s: (jnp.maximum(g - rows, 0), 0, 0)
                    ),
                ],
                out_specs=(out_block, out_block),
                scratch_shapes=[
                    pltpu.VMEM((tile, width), BF16),
                    pltpu.VMEM((columns, rows * terms, width), F32),
                    pltpu.VMEM((tiles, 2 * rows * terms, width), BF16),
                ],
            ),
            compiler_params=pltpu.CompilerParams(vmem_limit_bytes=40 * 1024 * 1024),
            cost_estimate=pl.CostEstimate(
                flops=8 * 2 * rows * columns * terms * tile * width // 2,
                bytes_accessed=8 * rows * columns * terms * tile,
                transcendentals=0,
            ),
            name="adjoint_product",
        )(scalars, *pieces, basis_rows, second_cols)

    waves = [split(wavefield, c) for c in range(CHUNKS)]
    gathered = [gather_pieces(w, "row") for w in waves]
    residuals, adjoints = [], []
    for c in range(CHUNKS):
        mine = gathered[c]
        pieces = mine + [swap("help", d, m) for d in range(1, helps) for m in mine]
        keep, send = run_forward(pieces)
        summed = keep + swap("help", 1, send).astype(F32)
        total = summed[0]
        for d in range(1, zs):
            total = total + swap("col", d, summed[d].astype(BF16)).astype(F32)
        weight = amplitude[..., c * part : (c + 1) * part].astype(F32)
        weight = jnp.concatenate([weight, weight], -1)
        resid = (weight * (total - split(observed, c).astype(F32))).astype(BF16)
        residuals.append(resid)
        mine = gather_pieces(resid, "col")
        pieces = mine + [swap("help", d, m) for d in range(1, helps) for m in mine]
        keep, send = run_adjoint(pieces)
        summed = keep + swap("help", 1, send).astype(F32)
        total = summed[0]
        for d in range(1, rs):
            total = total + swap("row", d, summed[d].astype(BF16)).astype(F32)
        adjoints.append(total.astype(BF16))

    def join(values):
        return jnp.stack(
            [
                jnp.concatenate([v[..., p * part : (p + 1) * part] for v in values], -1)
                for p in range(2)
            ]
        )

    return join(residuals), join(adjoints)


def solution(mesh):
    return jax.shard_map(
        body,
        mesh=mesh,
        in_specs=(
            P("freq", "col", ("row", "help"), None),
            P("freq", "row", "col", "help", None),
            P("freq", "row", "col", "help", None),
            P(("freq", "row"), "col"),
            P("freq", "row", ("col", "help"), None),
            P(("freq", "row"), ("col", "help"), None),
        ),
        out_specs=(
            P("freq", "row", ("col", "help"), None),
            P("freq", "col", ("row", "help"), None),
        ),
        check_vma=False,
    )
```

```python
import functools

import jax
import jax.numpy as jnp
from jax import lax
from jax.experimental import pallas as pl
from jax.experimental.pallas import tpu as pltpu
from jax.sharding import PartitionSpec as P

BF16 = jnp.bfloat16
F32 = jnp.float32
CHUNKS = 2
LANES = 128
VM = pl.BlockSpec(memory_space=pltpu.VMEM)
SM = pl.BlockSpec(memory_space=pltpu.SMEM)


def swap(axis_name, step, value):
    size = lax.axis_size(axis_name)
    return lax.ppermute(value, axis_name, [(i, i ^ step) for i in range(size)])


def turn(value, first, second):
    width = value.shape[-1]
    lane = lax.broadcasted_iota(jnp.int32, value.shape, value.ndim - 1)
    sign = jnp.where(lane < width // 2, first, second).astype(F32)
    return pltpu.roll(value, width // 2, value.ndim - 1) * sign


def forward_kernel(at_waves, at_ranks, at_z, helps, n_pieces, scalars, *refs):
    pieces = refs[:n_pieces]
    second, basis, keep_out, send_out, waves, coef, fwd = refs[n_pieces:]
    here = scalars[0]
    columns, quarter, width = pieces[0].shape
    rows = basis.shape[1]
    terms = second.shape[1] // (2 * rows)
    half = rows * terms
    row_index = lax.broadcasted_iota(jnp.int32, (terms, width), 0)
    for j in range(columns):
        for n, piece in enumerate(pieces):
            at = pl.multiple_of(scalars[at_waves + n] * quarter, quarter)
            waves[j, pl.ds(at, quarter), :] = piece[j]
        out = jnp.dot(second[j], waves[j], preferred_element_type=F32)
        value = out[:half] + turn(out[half:], 1.0, -1.0)
        for i in range(rows):
            left = scalars[at_ranks + i * columns + j] - here * terms
            part = value[i * terms : (i + 1) * terms]
            coef[i, j * terms : (j + 1) * terms, :] = jnp.where(row_index < left, part, 0.0)
    zs, _, span, _ = keep_out.shape
    dims = (((0,), (0,)), ((), ()))
    for i in range(rows):
        value = coef[i]
        turned = turn(value, -1.0, 1.0)
        out = lax.dot_general(value.astype(BF16), basis[0, i], dims, preferred_element_type=F32)
        out = out + lax.dot_general(turned.astype(BF16), basis[1, i], dims, preferred_element_type=F32)
        fwd[i] = out.T
        for z in range(zs):
            block = scalars[at_z + z] * helps
            at = pl.multiple_of((block + here) * span, span)
            keep_out[z, i] = fwd[i, pl.ds(at, span), :].astype(keep_out.dtype)
            at = pl.multiple_of((block + 1 - here) * span, span)
            send_out[z, i] = fwd[i, pl.ds(at, span), :].astype(send_out.dtype)


def adjoint_kernel(at_resid, at_ranks, at_r, helps, n_pieces, scalars, *refs):
    pieces = refs[:n_pieces]
    basis, second, keep_out, send_out, resid, back = refs[n_pieces:]
    here = scalars[0]
    blocks, rows, span, width = pieces[0].shape
    columns = second.shape[0]
    terms = second.shape[1] // (2 * rows)
    row_index = lax.broadcasted_iota(jnp.int32, (terms, width), 0)
    for i in range(rows):
        for n, piece in enumerate(pieces):
            for e in range(blocks):
                at = pl.multiple_of(scalars[at_resid + n * blocks + e] * span, span)
                resid[i, pl.ds(at, span), :] = piece[e, i]
        value = resid[i]
        turned = turn(value.astype(F32), 1.0, -1.0).astype(BF16)
        out = jnp.dot(basis[0, i], value, preferred_element_type=F32)
        out = out + jnp.dot(basis[1, i], turned, preferred_element_type=F32)
        for j in range(columns):
            left = scalars[at_ranks + i * columns + j] - here * terms
            part = out[j * terms : (j + 1) * terms]
            back[j, i * terms : (i + 1) * terms, :] = jnp.where(row_index < left, part, 0.0)
    rs, _, _, quarter = keep_out.shape
    for j in range(columns):
        value = back[j]
        left = jnp.concatenate([value, turn(value, -1.0, 1.0)], 0).T.astype(BF16)
        if quarter % LANES == 0:
            for out_ref, h in ((keep_out, here), (send_out, 1 - here)):
                for r in range(rs):
                    at = pl.multiple_of((scalars[at_r + r] * helps + h) * quarter, quarter)
                    out = jnp.dot(left, second[j, :, pl.ds(at, quarter)], preferred_element_type=F32)
                    out_ref[r, j] = out.astype(out_ref.dtype)
        else:
            out = jnp.dot(left, second[j], preferred_element_type=F32)
            for r in range(rs):
                for h in range(helps):
                    part = out[:, (r * helps + h) * quarter : (r * helps + h + 1) * quarter]
                    to = r ^ scalars[at_r]

                    @pl.when(here == h)
                    def _(part=part, to=to):
                        keep_out[to, j] = part.astype(keep_out.dtype)

                    @pl.when(here != h)
                    def _(part=part, to=to):
                        send_out[to, j] = part.astype(send_out.dtype)


def final_kernel(n_each, *refs):
    out_ref = refs[-1]
    groups = [refs[k : k + n_each] for k in range(0, len(refs) - 1, n_each)]
    part = groups[0][0].shape[1] // 2
    for j in range(out_ref.shape[1]):
        for p in range(2):
            pieces = []
            for group in groups:
                total = group[0][j, p * part : (p + 1) * part, :]
                for ref in group[1:]:
                    total = total + ref[j, p * part : (p + 1) * part, :].astype(F32)
                pieces.append(total)
            out_ref[p, j] = jnp.concatenate(pieces, 0).T.astype(out_ref.dtype)


def body(wavefield, basis_factor, second_factor, tile_ranks, observed, amplitude):
    _, columns, quarter, rhs = wavefield.shape
    _, rows, _, terms, tile = basis_factor.shape
    span = observed.shape[2]
    zs, rs, helps = lax.axis_size("col"), lax.axis_size("row"), lax.axis_size("help")
    z, r, h = lax.axis_index("col"), lax.axis_index("row"), lax.axis_index("help")
    part = rhs // CHUNKS
    width = 2 * part
    bits = zs.bit_length() - 1
    far = zs // 2
    near = [1 << b for b in range(bits - 1)]

    z_offsets = [int(format(n, f"0{bits}b")[::-1], 2) for n in range(zs)]
    r_offsets = list(range(rs))
    wave_places = [(r ^ d) * helps + (h ^ e) for e in range(helps) for d in r_offsets]
    z_places = [z ^ d for d in z_offsets]
    r_places = [r ^ d for d in r_offsets]
    offsets = [0]
    for d in reversed(near):
        offsets = offsets + [o ^ d for o in offsets]
    resid_places = [
        (z ^ o ^ f) * helps + (h ^ e) for e in range(helps) for o in offsets for f in (0, far)
    ]
    head = [h] + wave_places + z_places + resid_places + r_places
    at_waves = 1
    at_z = at_waves + len(wave_places)
    at_resid = at_z + len(z_places)
    at_r = at_resid + len(resid_places)
    at_ranks = at_r + len(r_places)
    scalars = jnp.concatenate([jnp.stack(head).astype(jnp.int32), tile_ranks.reshape(-1)])

    def split(value, c):
        return jnp.concatenate(
            [value[0, ..., c * part : (c + 1) * part], value[1, ..., c * part : (c + 1) * part]], -1
        )

    second_rows = second_factor.transpose(2, 0, 1, 3, 4).reshape(columns, 2 * rows * terms, tile)
    basis_rows = basis_factor.reshape(2, rows, columns * terms, tile)
    params = pltpu.CompilerParams(vmem_limit_bytes=20 * 1024 * 1024)
    cost = pl.CostEstimate(flops=4 * 10**9, bytes_accessed=10**6, transcendentals=0)

    def run_forward(pieces):
        shape = (zs, rows, span, width)
        return pl.pallas_call(
            functools.partial(forward_kernel, at_waves, at_ranks, at_z, helps, len(pieces)),
            out_shape=(jax.ShapeDtypeStruct(shape, F32), jax.ShapeDtypeStruct(shape, BF16)),
            in_specs=[SM] + [VM] * (len(pieces) + 2),
            out_specs=(VM, VM),
            scratch_shapes=[
                pltpu.VMEM((columns, tile, width), BF16),
                pltpu.VMEM((rows, columns * terms, width), F32),
                pltpu.VMEM((rows, tile, width), F32),
            ],
            compiler_params=params,
            cost_estimate=cost,
            name="forward_product",
        )(scalars, *pieces, second_rows, basis_rows)

    def run_adjoint(pieces):
        shape = (rs, columns, width, quarter)
        return pl.pallas_call(
            functools.partial(adjoint_kernel, at_resid, at_ranks, at_r, helps, len(pieces)),
            out_shape=(jax.ShapeDtypeStruct(shape, F32), jax.ShapeDtypeStruct(shape, BF16)),
            in_specs=[SM] + [VM] * (len(pieces) + 2),
            out_specs=(VM, VM),
            scratch_shapes=[
                pltpu.VMEM((rows, tile, width), BF16),
                pltpu.VMEM((columns, rows * terms, width), F32),
            ],
            compiler_params=params,
            cost_estimate=cost,
            name="adjoint_product",
        )(scalars, *pieces, basis_rows, second_rows)

    def share(pieces):
        return pieces + [swap("help", d, m) for d in range(1, helps) for m in pieces]

    waves = [split(wavefield, c) for c in range(CHUNKS)]
    gathered = [[w] + [swap("row", d, w) for d in range(1, rs)] for w in waves]
    data = jnp.concatenate([observed, amplitude[None]], 0)
    data = jnp.stack([data, swap("col", far, data)], 1).astype(F32)

    residuals, ends = [], []
    for c in range(CHUNKS):
        keep, send = run_forward(share(gathered[c]))
        total = keep + swap("help", 1, send).astype(F32)
        for d in near:
            n = total.shape[0] // 2
            total = total[:n] + swap("col", d, total[n:].astype(BF16)).astype(F32)
        total = total + swap("col", far, total[::-1].astype(BF16)).astype(F32)
        weight = data[2, ..., c * part : (c + 1) * part]
        weight = jnp.concatenate([weight, weight], -1)
        resid = (weight * (total - split(data[:2], c))).astype(BF16)
        residuals.append(resid[0])
        pieces = [resid]
        for d in reversed(near):
            pieces = pieces + [swap("col", d, m) for m in pieces]
        keep, send = run_adjoint(share(pieces))
        total = keep + swap("help", 1, send).astype(F32)
        ends += [total[0]] + [swap("row", d, total[d].astype(BF16)) for d in range(1, rs)]

    adjoint = pl.pallas_call(
        functools.partial(final_kernel, rs),
        out_shape=jax.ShapeDtypeStruct(wavefield.shape, BF16),
        in_specs=[VM] * len(ends),
        out_specs=VM,
        compiler_params=params,
        cost_estimate=pl.CostEstimate(flops=10**9, bytes_accessed=10**6, transcendentals=0),
        name="adjoint_sum",
    )(*ends)
    residual = jnp.stack(
        [jnp.concatenate([v[..., p * part : (p + 1) * part] for v in residuals], -1) for p in range(2)]
    )
    return residual, adjoint


def solution(mesh):
    return jax.shard_map(
        body,
        mesh=mesh,
        in_specs=(
            P("freq", "col", ("row", "help"), None),
            P("freq", "row", "col", "help", None),
            P("freq", "row", "col", "help", None),
            P(("freq", "row"), "col"),
            P("freq", "row", ("col", "help"), None),
            P(("freq", "row"), ("col", "help"), None),
        ),
        out_specs=(
            P("freq", "row", ("col", "help"), None),
            P("freq", "col", ("row", "help"), None),
        ),
        check_vma=False,
    )
```

```python
import functools

import jax
import jax.numpy as jnp
from jax import lax
from jax.experimental import pallas as pl
from jax.experimental.pallas import tpu as pltpu
from jax.sharding import PartitionSpec as P

BF16 = jnp.bfloat16
F32 = jnp.float32
CHUNKS = 2
LANES = 128
VM = pl.BlockSpec(memory_space=pltpu.VMEM)
SM = pl.BlockSpec(memory_space=pltpu.SMEM)
ANY = pl.BlockSpec(memory_space=pl.ANY)
MIB = 1024 * 1024
LARGE = 10**10
SPLIT = 2


def call(kernel, name, outs, ins, in_specs=None, scratch=(), limit=6 * MIB, cost=10**6):
    return pl.pallas_call(
        kernel,
        out_shape=[jax.ShapeDtypeStruct(shape, kind) for shape, kind in outs],
        in_specs=in_specs or [VM] * len(ins),
        out_specs=[VM] * len(outs),
        scratch_shapes=list(scratch),
        compiler_params=pltpu.CompilerParams(vmem_limit_bytes=limit),
        cost_estimate=pl.CostEstimate(flops=cost, bytes_accessed=10**4, transcendentals=0),
        name=name,
    )(*ins)


def swap(axis_name, step, value):
    size = lax.axis_size(axis_name)
    return lax.ppermute(value, axis_name, [(i, i ^ step) for i in range(size)])


def after(value, *earlier):
    return lax.optimization_barrier((value, *earlier))[0]


def turn(value, first, second):
    width = value.shape[-1]
    lane = lax.broadcasted_iota(jnp.int32, value.shape, value.ndim - 1)
    sign = jnp.where(lane < width // 2, first, second).astype(F32)
    return pltpu.roll(value, width // 2, value.ndim - 1) * sign


def waves_kernel(source, *outs):
    part = source.shape[-1] // len(outs)
    for j in range(source.shape[1]):
        for c, out in enumerate(outs):
            lanes = slice(c * part, (c + 1) * part)
            out[j] = jnp.concatenate([source[0, j, :, lanes], source[1, j, :, lanes]], -1)


def load_kernel(second_in, basis_in, second, basis, sems):
    rows = second_in.shape[1]
    copies = []
    for p in range(2):
        for i in range(rows):
            n = p * rows + i
            copies.append(pltpu.make_async_copy(second_in.at[p, i], second.at[:, n], sems.at[0, n]))
            copies.append(pltpu.make_async_copy(basis_in.at[p, i], basis.at[p, i], sems.at[1, n]))
    for copy in copies:
        copy.start()
    for copy in copies:
        copy.wait()


def halve_kernel(mine, other, keep, send):
    n = keep.shape[0]
    keep[...] = mine[:n] + other[:n].astype(F32)
    send[...] = (mine[n:] + other[n:].astype(F32)).astype(BF16)


def mirror_kernel(mine, other, keep, send):
    total = mine[...] + other[...].astype(F32)
    keep[...] = total
    n = keep.shape[0]
    for e in range(n):
        send[e] = total[n - 1 - e].astype(BF16)


def residual_kernel(c, mine, other, *refs):
    observed, amplitude, out = refs[:2], refs[2:4], refs[4]
    part = out.shape[-1] // 2
    lanes = slice(c * part, (c + 1) * part)
    for e in range(2):
        total = mine[e] + other[e].astype(F32)
        data = jnp.concatenate([observed[e][0, :, :, lanes], observed[e][1, :, :, lanes]], -1)
        weight = jnp.concatenate([amplitude[e][:, :, lanes]] * 2, -1)
        out[e] = (weight.astype(F32) * (total - data.astype(F32))).astype(BF16)


def join_kernel(*refs):
    out = refs[-1]
    part = out.shape[-1] // (len(refs) - 1)
    for p in range(2):
        out[p] = jnp.concatenate([ref[0, :, :, p * part : (p + 1) * part] for ref in refs[:-1]], -1)


def share_kernel(mine, *refs):
    others, out = refs[:-1], refs[-1]
    n = out.shape[0] // len(others)
    for k, other in enumerate(others):
        out[k * n : (k + 1) * n] = (mine[k * n : (k + 1) * n] + other[...].astype(F32)).astype(BF16)


def total_kernel(mine, *refs):
    others, out = refs[:-1], refs[-1]
    first, rest = others[:SPLIT], others[SPLIT:]
    n = out.shape[0] // len(first)
    for k, other in enumerate(first):
        total = mine[k * n : (k + 1) * n] + other[...].astype(F32)
        for ref in rest:
            total = total + ref[k * n : (k + 1) * n].astype(F32)
        out[k * n : (k + 1) * n] = total


def final_kernel(*refs):
    *done, mine = refs[: CHUNKS]
    others, out_ref = refs[CHUNKS:-1], refs[-1]
    first, rest = others[:SPLIT], others[SPLIT:]
    part = mine.shape[1] // 2
    n = mine.shape[0] // SPLIT
    for j in range(out_ref.shape[1]):
        for p in range(2):
            lanes = slice(p * part, (p + 1) * part)
            total = mine[j, lanes, :] + first[j // n][j % n, lanes, :].astype(F32)
            for ref in rest:
                total = total + ref[j, lanes, :].astype(F32)
            pieces = [ref[j, lanes, :] for ref in done] + [total]
            out_ref[p, j] = jnp.concatenate(pieces, 0).T.astype(out_ref.dtype)


def forward_kernel(rs, helps, z_offsets, ranks, *refs):
    n_pieces = rs * helps
    pieces = refs[:n_pieces]
    second, basis, keep_out, send_out, waves, coef, fwd = refs[n_pieces:]
    z, r, here = lax.axis_index("col"), lax.axis_index("row"), lax.axis_index("help")
    columns, quarter, width = pieces[0].shape
    rows = basis.shape[1]
    terms = second.shape[1] // (2 * rows)
    half = rows * terms
    row_index = lax.broadcasted_iota(jnp.int32, (terms, width), 0)
    for j in range(columns):
        for n, piece in enumerate(pieces):
            spot = (r ^ (n % rs)) * helps + (here ^ (n // rs))
            waves[j, pl.ds(pl.multiple_of(spot * quarter, quarter), quarter), :] = piece[j]
        out = jnp.dot(second[j], waves[j], preferred_element_type=F32)
        value = out[:half] + turn(out[half:], 1.0, -1.0)
        for i in range(rows):
            left = ranks[i, j] - here * terms
            part = value[i * terms : (i + 1) * terms]
            coef[i, j * terms : (j + 1) * terms, :] = jnp.where(row_index < left, part, 0.0)
    _, _, span, _ = keep_out.shape
    dims = (((0,), (0,)), ((), ()))
    for i in range(rows):
        value = coef[i]
        turned = turn(value, -1.0, 1.0)
        out = lax.dot_general(value.astype(BF16), basis[0, i], dims, preferred_element_type=F32)
        out = out + lax.dot_general(turned.astype(BF16), basis[1, i], dims, preferred_element_type=F32)
        fwd[i] = out.T
        for n, offset in enumerate(z_offsets):
            block = (z ^ offset) * helps
            at = pl.multiple_of((block + here) * span, span)
            keep_out[n, i] = fwd[i, pl.ds(at, span), :].astype(keep_out.dtype)
            at = pl.multiple_of((block + 1 - here) * span, span)
            send_out[n, i] = fwd[i, pl.ds(at, span), :].astype(send_out.dtype)


def adjoint_kernel(rs, helps, spots, ranks, *refs):
    n_pieces = len(spots)
    pieces, (basis, second) = refs[:n_pieces], refs[n_pieces : n_pieces + 2]
    keeps, sends = refs[n_pieces + 2 : n_pieces + 2 + rs], refs[n_pieces + 2 + rs : -2]
    resid, back = refs[-2:]
    z, r, here = lax.axis_index("col"), lax.axis_index("row"), lax.axis_index("help")
    blocks, rows, span, width = pieces[0].shape
    columns = second.shape[0]
    terms = second.shape[1] // (2 * rows)
    row_index = lax.broadcasted_iota(jnp.int32, (terms, width), 0)
    for i in range(rows):
        for piece, (z_offsets, h_offset) in zip(pieces, spots):
            for e, offset in enumerate(z_offsets):
                spot = (z ^ offset) * helps + (here ^ h_offset)
                resid[i, pl.ds(pl.multiple_of(spot * span, span), span), :] = piece[e, i]
        value = resid[i]
        turned = turn(value.astype(F32), 1.0, -1.0).astype(BF16)
        out = jnp.dot(basis[0, i], value, preferred_element_type=F32)
        out = out + jnp.dot(basis[1, i], turned, preferred_element_type=F32)
        for j in range(columns):
            left = ranks[i, j] - here * terms
            part = out[j * terms : (j + 1) * terms]
            back[j, i * terms : (i + 1) * terms, :] = jnp.where(row_index < left, part, 0.0)
    quarter = keeps[0].shape[2]

    def keep(d, j, value):
        keeps[d][j] = value

    def send(d, j, value):
        refs = sends[d * SPLIT : (d + 1) * SPLIT]
        n = refs[0].shape[0]
        refs[j // n][j % n] = value.astype(BF16)

    for j in range(columns):
        value = back[j]
        left = jnp.concatenate([value, turn(value, -1.0, 1.0)], 0).T.astype(BF16)
        if quarter % LANES == 0:
            for put, h in ((keep, here), (send, 1 - here)):
                for d in range(rs):
                    at = pl.multiple_of(((r ^ d) * helps + h) * quarter, quarter)
                    out = jnp.dot(left, second[j, :, pl.ds(at, quarter)], preferred_element_type=F32)
                    put(d, j, out)
        else:
            out = jnp.dot(left, second[j], preferred_element_type=F32)
            for n in range(rs):
                for h in range(helps):
                    part = out[:, (n * helps + h) * quarter : (n * helps + h + 1) * quarter]
                    for d in range(rs):
                        pl.when((here == h) & (n ^ r == d))(functools.partial(keep, d, j, part))
                        pl.when((here != h) & (n ^ r == d))(functools.partial(send, d, j, part))


def body(wavefield, basis_factor, second_factor, tile_ranks, observed, amplitude):
    _, columns, quarter, rhs = wavefield.shape
    _, rows, _, terms, tile = basis_factor.shape
    span = observed.shape[2]
    zs, rs, helps = lax.axis_size("col"), lax.axis_size("row"), lax.axis_size("help")
    width = 2 * rhs // CHUNKS
    bits = zs.bit_length() - 1
    far = zs // 2
    near = [1 << b for b in range(bits - 1)]
    z_offsets = [int(format(n, f"0{bits}b")[::-1], 2) for n in range(zs)]

    def share(pieces):
        return pieces + [swap("help", d, m) for d in range(1, helps) for m in pieces]

    waves = call(
        waves_kernel, "split_waves", [((columns, quarter, width), BF16)] * CHUNKS, [wavefield]
    )
    gathered = [[w] + [swap("row", d, w) for d in range(1, rs)] for w in waves]
    data = [observed, swap("col", far, observed), amplitude, swap("col", far, amplitude)]
    second, basis = call(
        load_kernel,
        "load_factors",
        [((columns, 2 * rows, terms, tile), BF16), ((2, rows, columns, terms, tile), BF16)],
        [second_factor, basis_factor],
        in_specs=[pl.BlockSpec(memory_space=pltpu.HBM)] * 2,
        scratch=[pltpu.SemaphoreType.DMA((2, 2 * rows))],
        cost=LARGE,
    )
    second = second.reshape(columns, 2 * rows * terms, tile)
    basis = basis.reshape(2, rows, columns * terms, tile)

    def forward(c, mine):
        shape = (zs, rows, span, width)
        pieces = share(mine)
        return call(
            functools.partial(forward_kernel, rs, helps, z_offsets),
            "forward_product",
            [(shape, F32), (shape, BF16)],
            [tile_ranks, *pieces, second, basis],
            in_specs=[SM] + [VM] * (len(pieces) + 2),
            scratch=[
                pltpu.VMEM((columns, tile, width), BF16),
                pltpu.VMEM((rows, columns * terms, width), F32),
                pltpu.VMEM((rows, tile, width), F32),
            ],
            limit=16 * MIB,
            cost=LARGE if c else 1,
        )

    def backward(pieces, spots):
        whole, piece = (columns, width, quarter), (columns // SPLIT, width, quarter)
        outs = call(
            functools.partial(adjoint_kernel, rs, helps, spots),
            "adjoint_product",
            [(whole, F32)] * rs + [(piece, BF16)] * (rs * SPLIT),
            [tile_ranks, *pieces, basis, second],
            in_specs=[SM] + [VM] * (len(pieces) + 2),
            scratch=[
                pltpu.VMEM((rows, tile, width), BF16),
                pltpu.VMEM((columns, rows * terms, width), F32),
            ],
            limit=16 * MIB,
            cost=LARGE,
        )
        sends = outs[rs:]
        return outs[:rs], [sends[d * SPLIT : (d + 1) * SPLIT] for d in range(rs)]

    halved, mirrored, residuals, shared, totals = [], [], [], [], []

    def front(c):
        earlier = (halved[-1],) if c else (second, data[1], data[3])
        mine = [gathered[c][0]] + [after(m, *earlier) for m in gathered[c][1:]]
        if c:
            mine[0] = after(mine[0], mirrored[-1][1])
        keep, send = forward(c, mine)
        if c:
            residual_of(c - 1, send)
            keep = after(keep, residuals[c - 1])
        other = swap("help", 1, send)
        for d in near:
            shape = (keep.shape[0] // 2, rows, span, width)
            keep, send = call(
                halve_kernel, "halve", [(shape, F32), (shape, BF16)], [keep, other], cost=LARGE if c else 1
            )
            other = swap("col", d, send)
        halved.append(send)
        mirrored.append(call(mirror_kernel, "mirror", [(shape, F32), (shape, BF16)], [keep, other]))

    def residual_of(c, *earlier):
        keep, send = mirrored[c]
        residuals.extend(
            call(
                functools.partial(residual_kernel, c),
                "residual",
                [((2, rows, span, width), BF16)],
                [after(keep, *earlier), swap("col", far, send), *data],
                cost=LARGE,
            )
        )

    def rear(c):
        pieces, offsets = [residuals[c]], [0]
        for d in reversed(near):
            pieces = pieces + [swap("col", d, m) for m in pieces]
            offsets = offsets + [o ^ d for o in offsets]
        pieces = share(pieces)
        spots = [((o, o ^ far), e) for e in range(helps) for o in offsets]
        last = c + 1 == CHUNKS
        pieces[0] = after(pieces[0], *(shared[-1] if last else [mirrored[c + 1][1]]))
        keeps, sends = backward(pieces, spots)
        if not last:
            residual_of(c + 1, sends[-1][-1])
            keeps = [keeps[0]] + [after(k, residuals[c + 1]) for k in keeps[1:]]
        shape = (columns, width, quarter)
        shared.append(
            [
                call(
                    share_kernel, "adjoint_share", [(shape, BF16)], [k, *[swap("help", 1, m) for m in s]]
                )[0]
                for k, s in zip(keeps[1:], sends[1:])
            ]
        )
        if last:
            totals[-1] = [after(totals[-1][0], *shared[-1])] + totals[-1][1:]
            totals[-1] = call(total_kernel, "total", [(shape, F32)], totals[-1], cost=LARGE)
        totals.append(
            [keeps[0], *[swap("help", 1, m) for m in sends[0]]]
            + [swap("row", d + 1, m) for d, m in enumerate(shared[-1])]
        )

    for c in range(CHUNKS):
        front(c)
    for c in range(CHUNKS):
        rear(c)

    residual = call(join_kernel, "join", [(observed.shape, BF16)], residuals, cost=LARGE)[0]
    adjoint = call(
        final_kernel, "adjoint_sum", [(wavefield.shape, BF16)], [*totals[0], *totals[1]]
    )[0]
    return residual, adjoint


def solution(mesh):
    return jax.shard_map(
        body,
        mesh=mesh,
        in_specs=(
            P("freq", "col", ("row", "help"), None),
            P("freq", "row", "col", "help", None),
            P("freq", "row", "col", "help", None),
            P(("freq", "row"), "col"),
            P("freq", "row", ("col", "help"), None),
            P(("freq", "row"), ("col", "help"), None),
        ),
        out_specs=(
            P("freq", "row", ("col", "help"), None),
            P("freq", "col", ("row", "help"), None),
        ),
        check_vma=False,
    )
```

```python
import functools

import jax
import jax.numpy as jnp
from jax import lax
from jax.experimental import pallas as pl
from jax.experimental.pallas import tpu as pltpu
from jax.sharding import PartitionSpec as P

BF16 = jnp.bfloat16
F32 = jnp.float32
CHUNKS = 2
LANES = 128
VM = pl.BlockSpec(memory_space=pltpu.VMEM)
SM = pl.BlockSpec(memory_space=pltpu.SMEM)
ANY = pl.BlockSpec(memory_space=pl.ANY)
MIB = 1024 * 1024
LARGE = 10**10
SPLIT = 2


def call(kernel, name, outs, ins, in_specs=None, scratch=(), limit=6 * MIB, cost=10**6):
    return pl.pallas_call(
        kernel,
        out_shape=[jax.ShapeDtypeStruct(shape, kind) for shape, kind in outs],
        in_specs=in_specs or [VM] * len(ins),
        out_specs=[VM] * len(outs),
        scratch_shapes=list(scratch),
        compiler_params=pltpu.CompilerParams(vmem_limit_bytes=limit),
        cost_estimate=pl.CostEstimate(flops=cost, bytes_accessed=10**4, transcendentals=0),
        name=name,
    )(*ins)


def swap(axis_name, step, value):
    size = lax.axis_size(axis_name)
    return lax.ppermute(value, axis_name, [(i, i ^ step) for i in range(size)])


def after(value, *earlier):
    return lax.optimization_barrier((value, *earlier))[0]


def turn(value, first, second):
    width = value.shape[-1]
    lane = lax.broadcasted_iota(jnp.int32, value.shape, value.ndim - 1)
    sign = jnp.where(lane < width // 2, first, second).astype(F32)
    return pltpu.roll(value, width // 2, value.ndim - 1) * sign


def waves_kernel(source, *outs):
    part = outs[0].shape[-1] // 2
    at = 0
    for out in outs:
        for j in range(out.shape[0]):
            c, row = divmod(at, source.shape[1])
            lanes = slice(c * part, (c + 1) * part)
            out[j] = jnp.concatenate([source[0, row, :, lanes], source[1, row, :, lanes]], -1)
            at += 1


def load_kernel(second_in, basis_in, second, basis, sems):
    rows = second_in.shape[1]
    copies = []
    for p in range(2):
        for i in range(rows):
            n = p * rows + i
            copies.append(pltpu.make_async_copy(second_in.at[p, i], second.at[:, n], sems.at[0, n]))
            copies.append(pltpu.make_async_copy(basis_in.at[p, i], basis.at[p, i], sems.at[1, n]))
    for copy in copies:
        copy.start()
    for copy in copies:
        copy.wait()


def halve_kernel(mine, *refs):
    others, keep, send = refs[:-2], refs[-2], refs[-1]
    n = keep.shape[0]
    total = jnp.concatenate([other[...] for other in others], 0).astype(F32) + mine[...]
    keep[...] = total[:n]
    send[...] = total[n:].astype(BF16)


def mirror_kernel(mine, *refs):
    others, keep, send = refs[:-2], refs[-2], refs[-1]
    total = jnp.concatenate([other[...] for other in others], 0).astype(F32) + mine[...]
    keep[...] = total
    n = keep.shape[0]
    for e in range(n):
        send[e] = total[n - 1 - e].astype(BF16)


def residual_kernel(c, mine, other, *refs):
    observed, amplitude, out = refs[:2], refs[2:4], refs[4]
    part = out.shape[-1] // 2
    lanes = slice(c * part, (c + 1) * part)
    for e in range(2):
        total = mine[e] + other[e].astype(F32)
        data = jnp.concatenate([observed[e][0, :, :, lanes], observed[e][1, :, :, lanes]], -1)
        weight = jnp.concatenate([amplitude[e][:, :, lanes]] * 2, -1)
        out[e] = (weight.astype(F32) * (total - data.astype(F32))).astype(BF16)


def join_kernel(*refs):
    out = refs[-1]
    part = out.shape[-1] // (len(refs) - 1)
    for p in range(2):
        out[p] = jnp.concatenate([ref[0, :, :, p * part : (p + 1) * part] for ref in refs[:-1]], -1)


def share_kernel(mine, *refs):
    others, out = refs[:-1], refs[-1]
    n = others[0].shape[0]
    for k, other in enumerate(others):
        at = slice(k * n, (k + 1) * n)
        out[at] = (mine[at] + other[...].astype(F32)).astype(BF16)


def total_kernel(mine, *refs):
    others, out = refs[:-1], refs[-1]
    total = mine[...]
    for ref in others:
        total = total + ref[...].astype(F32)
    out[...] = total


def final_kernel(done, mine, *refs):
    others, out_ref = refs[:-1], refs[-1]
    part = mine.shape[1] // 2
    for j in range(out_ref.shape[1]):
        for p in range(2):
            lanes = slice(p * part, (p + 1) * part)
            total = mine[j, lanes, :]
            for ref in others:
                total = total + ref[j, lanes, :].astype(F32)
            out_ref[p, j] = jnp.concatenate([done[j, lanes, :], total], 0).T.astype(out_ref.dtype)


def forward_kernel(rs, helps, z_offsets, n_groups, ranks, *refs):
    n_pieces = rs * helps
    groups = [refs[k * n_pieces : (k + 1) * n_pieces] for k in range(n_groups)]
    second, basis, keep_out, *sends, waves, coef, fwd = refs[n_groups * n_pieces :]
    n_send = sends[0].shape[0]
    z, r, here = lax.axis_index("col"), lax.axis_index("row"), lax.axis_index("help")
    _, quarter, width = groups[0][0].shape
    spots = [(group, j) for group in groups for j in range(group[0].shape[0])]
    columns = len(spots)
    rows = basis.shape[1]
    terms = second.shape[1] // (2 * rows)
    half = rows * terms
    row_index = lax.broadcasted_iota(jnp.int32, (terms, width), 0)
    places = [((r ^ (n % rs)) * helps + (here ^ (n // rs))) * quarter for n in range(n_pieces)]
    places = [pl.multiple_of(at, quarter) for at in places]
    for j, (group, at_j) in enumerate(spots):
        if quarter % LANES == 0:
            left = jnp.concatenate([second[j, :, pl.ds(at, quarter)] for at in places], 1)
            right = jnp.concatenate([piece[at_j] for piece in group], 0)
        else:
            for at, piece in zip(places, group):
                waves[j, pl.ds(at, quarter), :] = piece[at_j]
            left, right = second[j], waves[j]
        out = jnp.dot(left, right, preferred_element_type=F32)
        value = out[:half] + turn(out[half:], 1.0, -1.0)
        for i in range(rows):
            left = ranks[i, j] - here * terms
            part = value[i * terms : (i + 1) * terms]
            coef[i, j * terms : (j + 1) * terms, :] = jnp.where(row_index < left, part, 0.0)
    _, _, span, _ = keep_out.shape
    dims = (((0,), (0,)), ((), ()))
    for i in range(rows):
        value = coef[i]
        left = jnp.concatenate([value, turn(value, -1.0, 1.0)], 0).astype(BF16)
        right = jnp.concatenate([basis[0, i], basis[1, i]], 0)
        out = lax.dot_general(left, right, dims, preferred_element_type=F32)
        fwd[i] = out.T
        for n, offset in enumerate(z_offsets):
            block = (z ^ offset) * helps
            at = pl.multiple_of((block + here) * span, span)
            keep_out[n, i] = fwd[i, pl.ds(at, span), :].astype(keep_out.dtype)
            at = pl.multiple_of((block + 1 - here) * span, span)
            sends[n // n_send][n % n_send, i] = fwd[i, pl.ds(at, span), :].astype(BF16)


def adjoint_kernel(rs, helps, spots, ranks, *refs):
    n_pieces = len(spots)
    pieces, (basis, second) = refs[:n_pieces], refs[n_pieces : n_pieces + 2]
    keeps, sends = refs[n_pieces + 2 : n_pieces + 2 + rs], refs[n_pieces + 2 + rs : -2]
    resid, back = refs[-2:]
    z, r, here = lax.axis_index("col"), lax.axis_index("row"), lax.axis_index("help")
    blocks, rows, span, width = pieces[0].shape
    columns = second.shape[0]
    terms = second.shape[1] // (2 * rows)
    row_index = lax.broadcasted_iota(jnp.int32, (terms, width), 0)
    for i in range(rows):
        for piece, (z_offsets, h_offset) in zip(pieces, spots):
            for e, offset in enumerate(z_offsets):
                spot = (z ^ offset) * helps + (here ^ h_offset)
                resid[i, pl.ds(pl.multiple_of(spot * span, span), span), :] = piece[e, i]
        value = resid[i]
        turned = turn(value.astype(F32), 1.0, -1.0).astype(BF16)
        left = jnp.concatenate([basis[0, i], basis[1, i]], 1)
        out = jnp.dot(left, jnp.concatenate([value, turned], 0), preferred_element_type=F32)
        for j in range(columns):
            left = ranks[i, j] - here * terms
            part = out[j * terms : (j + 1) * terms]
            back[j, i * terms : (i + 1) * terms, :] = jnp.where(row_index < left, part, 0.0)
    quarter = keeps[0].shape[2]

    def keep(d, j, value):
        keeps[d][j] = value

    parts = (len(sends) - 1) // (rs - 1)

    def send(d, j, value):
        refs = sends[:1] if d == 0 else sends[1 + (d - 1) * parts : 1 + d * parts]
        n = refs[0].shape[0]
        refs[j // n][j % n] = value.astype(BF16)

    half = back.shape[1]
    for j in range(columns):
        real = back[j].astype(BF16).T
        turned = jnp.concatenate([-real[width // 2 :], real[: width // 2]], 0)

        def product(right):
            out = jnp.dot(real, right[:half], preferred_element_type=F32)
            return out + jnp.dot(turned, right[half:], preferred_element_type=F32)

        if quarter % LANES == 0:
            for put, h in ((keep, here), (send, 1 - here)):
                places = [((r ^ d) * helps + h) * quarter for d in range(rs)]
                places = [pl.multiple_of(at, quarter) for at in places]
                out = product(jnp.concatenate([second[j, :, pl.ds(at, quarter)] for at in places], 1))
                for d in range(rs):
                    put(d, j, out[:, d * quarter : (d + 1) * quarter])
        else:
            out = product(second[j])
            for n in range(rs):
                for h in range(helps):
                    part = out[:, (n * helps + h) * quarter : (n * helps + h + 1) * quarter]
                    for d in range(rs):
                        pl.when((here == h) & (n ^ r == d))(functools.partial(keep, d, j, part))
                        pl.when((here != h) & (n ^ r == d))(functools.partial(send, d, j, part))


def body(wavefield, basis_factor, second_factor, tile_ranks, observed, amplitude):
    _, columns, quarter, rhs = wavefield.shape
    _, rows, _, terms, tile = basis_factor.shape
    span = observed.shape[2]
    zs, rs, helps = lax.axis_size("col"), lax.axis_size("row"), lax.axis_size("help")
    width = 2 * rhs // CHUNKS
    bits = zs.bit_length() - 1
    far = zs // 2
    near = [1 << b for b in range(bits - 1)]
    z_offsets = [int(format(n, f"0{bits}b")[::-1], 2) for n in range(zs)]

    def share(pieces):
        return pieces + [swap("help", d, m) for d in range(1, helps) for m in pieces]

    sizes = [[5 * columns // 8, 3 * columns // 8]] + [[columns]] * (CHUNKS - 1)
    waves = call(
        waves_kernel,
        "split_waves",
        [((n, quarter, width), BF16) for ns in sizes for n in ns],
        [wavefield],
    )
    waves = [waves[:2]] + [[w] for w in waves[2:]]
    gathered = [[[w] + [swap("row", d, w) for d in range(1, rs)] for w in ws] for ws in waves]
    data = [observed, amplitude]
    data = [m for d in data for m in (d, swap("col", far, after(d, waves[0][0])))]
    second, basis = call(
        load_kernel,
        "load_factors",
        [((columns, 2 * rows, terms, tile), BF16), ((2, rows, columns, terms, tile), BF16)],
        [second_factor, basis_factor],
        in_specs=[pl.BlockSpec(memory_space=pltpu.HBM)] * 2,
        scratch=[pltpu.SemaphoreType.DMA((2, 2 * rows))],
        cost=LARGE,
    )
    second = second.reshape(columns, 2 * rows * terms, tile)
    basis = basis.reshape(2, rows, columns * terms, tile)

    def forward(c, mine):
        shape, piece = (zs, rows, span, width), (zs // SPLIT, rows, span, width)
        pieces = [m for group in mine for m in share(group)]
        return call(
            functools.partial(forward_kernel, rs, helps, z_offsets, len(mine)),
            "forward_product",
            [(shape, F32)] + [(piece, BF16)] * SPLIT,
            [tile_ranks, *pieces, second, basis],
            in_specs=[SM] + [VM] * (len(pieces) + 2),
            scratch=[
                pltpu.VMEM((columns, tile, width), BF16),
                pltpu.VMEM((rows, columns * terms, width), F32),
                pltpu.VMEM((rows, tile, width), F32),
            ],
            limit=16 * MIB,
            cost=LARGE if c else 1,
        )

    def backward(c, pieces, spots):
        whole = (columns, width, quarter)
        parts = 2
        piece = (columns // parts, width, quarter)
        outs = call(
            functools.partial(adjoint_kernel, rs, helps, spots),
            "adjoint_product",
            [(whole, F32)] * rs + [(whole, BF16)] + [(piece, BF16)] * ((rs - 1) * parts),
            [tile_ranks, *pieces, basis, second],
            in_specs=[SM] + [VM] * (len(pieces) + 2),
            scratch=[
                pltpu.VMEM((rows, tile, width), BF16),
                pltpu.VMEM((columns, rows * terms, width), F32),
            ],
            limit=16 * MIB,
            cost=1 if c + 1 == CHUNKS else LARGE,
        )
        sends = outs[rs:]
        return outs[:rs], [sends[:1]] + [sends[1 + d * parts : 1 + (d + 1) * parts] for d in range(rs - 1)]

    halved, mirrored, residuals, sent, totals = [], [], [], [], []

    def front(c):
        earlier = (mirrored[-1][1],) if c else (second, data[1], data[3])
        mine = [[group[0]] + [after(m, *earlier) for m in group[1:]] for group in gathered[c]]
        if c:
            mine[0][0] = after(mine[0][0], mirrored[-1][1])
        keep, *sends = forward(c, mine)
        if c:
            residual_of(c - 1, sends[-1])
            keep = after(keep, residuals[c - 1])
        others = [swap("help", 1, send) for send in sends]
        for d in near:
            shape = (keep.shape[0] // 2, rows, span, width)
            keep, send = call(
                halve_kernel, "halve", [(shape, F32), (shape, BF16)], [keep, *others], cost=LARGE if c else 1
            )
            others = [swap("col", d, send)]
        halved.append(send)
        mirrored.append(call(mirror_kernel, "mirror", [(shape, F32), (shape, BF16)], [keep, *others]))

    def residual_of(c, *earlier):
        keep, send = mirrored[c]
        residuals.extend(
            call(
                functools.partial(residual_kernel, c),
                "residual",
                [((2, rows, span, width), BF16)],
                [after(keep, *earlier), swap("col", far, send), *data],
                cost=LARGE,
            )
        )

    def rear(c):
        pieces, offsets = [residuals[c]], [0]
        for d in reversed(near):
            pieces = pieces + [swap("col", d, m) for m in pieces]
            offsets = offsets + [o ^ d for o in offsets]
        last = c + 1 == CHUNKS
        if last:
            pieces[1:] = [after(m, *sent) for m in pieces[1:]]
        pieces = share(pieces)
        spots = [((o, o ^ far), e) for e in range(helps) for o in offsets]
        if not last:
            pieces[0] = after(pieces[0], mirrored[c + 1][1])
        keeps, sends = backward(c, pieces, spots)
        if not last:
            residual_of(c + 1, sends[-1][-1])
            keeps = [keeps[0]] + [after(k, residuals[c + 1]) for k in keeps[1:]]
        shape = (columns, width, quarter)
        shared = [
            call(
                share_kernel,
                "adjoint_share",
                [(shape, BF16)],
                [k, *[swap("help", 1, m) for m in s]],
            )[0]
            for k, s in zip(keeps[1:], sends[1:])
        ]
        if last:
            totals[-1][0] = after(totals[-1][0], *shared)
            totals[-1] = call(total_kernel, "total", [(shape, F32)], totals[-1], cost=LARGE)
        else:
            sent.extend(shared)
        totals.append(
            [keeps[0], swap("help", 1, after(sends[0][0], *shared))]
            + [swap("row", d + 1, m) for d, m in enumerate(shared)]
        )

    for c in range(CHUNKS):
        front(c)
    for c in range(CHUNKS):
        rear(c)

    residual = call(join_kernel, "join", [(observed.shape, BF16)], residuals, cost=1)[0]
    adjoint = call(
        final_kernel, "adjoint_sum", [(wavefield.shape, BF16)], [*totals[0], *totals[1]]
    )[0]
    return residual, adjoint


def solution(mesh):
    return jax.shard_map(
        body,
        mesh=mesh,
        in_specs=(
            P("freq", "col", ("row", "help"), None),
            P("freq", "row", "col", "help", None),
            P("freq", "row", "col", "help", None),
            P(("freq", "row"), "col"),
            P("freq", "row", ("col", "help"), None),
            P(("freq", "row"), ("col", "help"), None),
        ),
        out_specs=(
            P("freq", "row", ("col", "help"), None),
            P("freq", "col", ("row", "help"), None),
        ),
        check_vma=False,
    )
```

```python
import functools

import jax
import jax.numpy as jnp
from jax import lax
from jax.experimental import pallas as pl
from jax.experimental.pallas import tpu as pltpu
from jax.sharding import PartitionSpec as P

BF16 = jnp.bfloat16
F32 = jnp.float32
CHUNKS = 2
LANES = 128
VM = pl.BlockSpec(memory_space=pltpu.VMEM)
SM = pl.BlockSpec(memory_space=pltpu.SMEM)
HBM = pl.BlockSpec(memory_space=pltpu.HBM)
ANY = pl.BlockSpec(memory_space=pl.ANY)
MIB = 1024 * 1024
LARGE = 10**10
SPLIT = 2
BLOCKS = (1, 2)


def call(kernel, name, outs, ins, in_specs=None, scratch=(), limit=6 * MIB, cost=10**6):
    return pl.pallas_call(
        kernel,
        out_shape=[jax.ShapeDtypeStruct(shape, kind) for shape, kind in outs],
        in_specs=in_specs or [VM] * len(ins),
        out_specs=[VM] * len(outs),
        scratch_shapes=list(scratch),
        compiler_params=pltpu.CompilerParams(vmem_limit_bytes=limit),
        cost_estimate=pl.CostEstimate(flops=cost, bytes_accessed=10**4, transcendentals=0),
        name=name,
    )(*ins)


def in_hbm(value):
    return pltpu.with_memory_space_constraint(value, pltpu.HBM)


def swap(axis_name, step, value):
    size = lax.axis_size(axis_name)
    return lax.ppermute(value, axis_name, [(i, i ^ step) for i in range(size)])


def after(value, *earlier):
    return lax.optimization_barrier((value, *earlier))[0]


def turn(value, first, second):
    width = value.shape[-1]
    lane = lax.broadcasted_iota(jnp.int32, value.shape, value.ndim - 1)
    sign = jnp.where(lane < width // 2, first, second).astype(F32)
    return pltpu.roll(value, width // 2, value.ndim - 1) * sign


def side_by_side(source, j, c, part):
    lanes = slice(c * part, (c + 1) * part)
    return jnp.concatenate([source[0, j, :, lanes], source[1, j, :, lanes]], -1)


def first_kernel(source, out, held, sems):
    n = out.shape[0]
    copies = [pltpu.make_async_copy(source.at[p, :n], held.at[p], sems.at[p]) for p in range(2)]
    for copy in copies:
        copy.start()
    for copy in copies:
        copy.wait()
    for j in range(n):
        out[j] = side_by_side(held, j, 0, out.shape[-1] // 2)


def waves_kernel(source, rest, whole, *others):
    columns, part = whole.shape[0], whole.shape[-1] // 2
    first = columns - rest.shape[0]
    for j in range(columns):
        whole[j] = side_by_side(source, j, 0, part)
        if j >= first:
            rest[j - first] = whole[j]
        for c, other in enumerate(others):
            other[j] = side_by_side(source, j, c + 1, part)


def data_kernel(observed, amplitude, out, sems):
    copies = [
        pltpu.make_async_copy(observed, out.at[:2], sems.at[0]),
        pltpu.make_async_copy(amplitude, out.at[2], sems.at[1]),
    ]
    for copy in copies:
        copy.start()
    for copy in copies:
        copy.wait()


def load_kernel(second_in, basis_in, second, basis, sems):
    rows = second_in.shape[1]
    copies = []
    for p in range(2):
        for i in range(rows):
            n = p * rows + i
            copies.append(pltpu.make_async_copy(second_in.at[p, i], second.at[:, n], sems.at[0, n]))
            copies.append(pltpu.make_async_copy(basis_in.at[p, i], basis.at[p, i], sems.at[1, n]))
    for copy in copies:
        copy.start()
    for copy in copies:
        copy.wait()


def halve_kernel(mine, *refs):
    others, keep, send = refs[:-2], refs[-2], refs[-1]
    n = keep.shape[0]
    total = jnp.concatenate([other[...] for other in others], 0).astype(F32) + mine[...]
    keep[...] = total[:n]
    send[...] = total[n:].astype(BF16)


def mirror_kernel(mine, *refs):
    others, keep, send = refs[:-2], refs[-2], refs[-1]
    total = jnp.concatenate([other[...] for other in others], 0).astype(F32) + mine[...]
    keep[...] = total
    n = keep.shape[0]
    for e in range(n):
        send[e] = total[n - 1 - e].astype(BF16)


def residual_kernel(c, mine, other, *refs):
    arrays, outs = refs[:2], refs[2:]
    part = outs[0].shape[-1] // 2
    lanes = slice(c * part, (c + 1) * part)
    for e in range(2):
        total = mine[e] + other[e].astype(F32)
        data = jnp.concatenate([arrays[e][p, :, :, lanes] for p in range(2)], -1)
        weight = jnp.concatenate([arrays[e][2, :, :, lanes]] * 2, -1)
        value = (weight.astype(F32) * (total - data.astype(F32))).astype(BF16)
        outs[e // outs[0].shape[0]][e % outs[0].shape[0]] = value


def join_kernel(*refs):
    out = refs[-1]
    part = out.shape[-1] // (len(refs) - 1)
    for p in range(2):
        out[p] = jnp.concatenate([ref[0, :, :, p * part : (p + 1) * part] for ref in refs[:-1]], -1)


def share_kernel(mine, *refs):
    others, out = refs[:-1], refs[-1]
    n = others[0].shape[0]
    for k, other in enumerate(others):
        at = slice(k * n, (k + 1) * n)
        out[at] = (mine[at] + other[...].astype(F32)).astype(BF16)


def total_kernel(mine, *refs):
    others, out = refs[:-1], refs[-1]
    total = mine[...]
    for ref in others:
        total = total + ref[...].astype(F32)
    out[...] = total


def final_kernel(done, mine, *refs):
    others, out_ref = refs[:-1], refs[-1]
    part = mine.shape[1] // 2
    for j in range(out_ref.shape[1]):
        for p in range(2):
            lanes = slice(p * part, (p + 1) * part)
            total = mine[j, lanes, :]
            for ref in others:
                total = total + ref[j, lanes, :].astype(F32)
            out_ref[p, j] = jnp.concatenate([done[j, lanes, :], total], 0).astype(out_ref.dtype).T


def forward_kernel(rs, helps, z_offsets, counts, ranks, *refs):
    n_pieces = rs * helps
    slots, at = [], 0
    for count in counts:
        slots.append([(ref, j) for ref in refs[at : at + count] for j in range(ref.shape[0])])
        at += count
    second, basis, keep_out, *sends, waves, coef, fwd = refs[at:]
    n_send = sends[0].shape[0]
    z, r, here = lax.axis_index("col"), lax.axis_index("row"), lax.axis_index("help")
    _, quarter, width = refs[0].shape
    columns = len(slots[0])
    rows = basis.shape[1]
    terms = second.shape[1] // (2 * rows)
    half = rows * terms
    row_index = lax.broadcasted_iota(jnp.int32, (terms, width), 0)
    places = [((r ^ (n % rs)) * helps + (here ^ (n // rs))) * quarter for n in range(n_pieces)]
    places = [pl.multiple_of(at, quarter) for at in places]
    for j in range(columns):
        parts = [ref[n] for ref, n in (slot[j] for slot in slots)]
        if quarter % LANES == 0:
            left = jnp.concatenate([second[j, :, pl.ds(at, quarter)] for at in places], 1)
            right = jnp.concatenate(parts, 0)
        else:
            for at, part in zip(places, parts):
                waves[j, pl.ds(at, quarter), :] = part
            left, right = second[j], waves[j]
        out = jnp.dot(left, right, preferred_element_type=F32)
        value = out[:half] + turn(out[half:], 1.0, -1.0)
        for i in range(rows):
            left = ranks[i, j] - here * terms
            part = value[i * terms : (i + 1) * terms]
            coef[i, j * terms : (j + 1) * terms, :] = jnp.where(row_index < left, part, 0.0)
    _, _, span, _ = keep_out.shape
    dims = (((0,), (0,)), ((), ()))
    for i in range(rows):
        value = coef[i]
        left = jnp.concatenate([value, turn(value, -1.0, 1.0)], 0).astype(BF16)
        right = jnp.concatenate([basis[0, i], basis[1, i]], 0)
        out = lax.dot_general(left, right, dims, preferred_element_type=F32)
        fwd[i] = out.T
        for n, offset in enumerate(z_offsets):
            block = (z ^ offset) * helps
            at = pl.multiple_of((block + here) * span, span)
            keep_out[n, i] = fwd[i, pl.ds(at, span), :].astype(keep_out.dtype)
            at = pl.multiple_of((block + 1 - here) * span, span)
            sends[n // n_send][n % n_send, i] = fwd[i, pl.ds(at, span), :].astype(BF16)


def adjoint_kernel(rs, helps, spots, ranks, *refs):
    n_pieces = len(spots)
    pieces, (basis, second) = refs[:n_pieces], refs[n_pieces : n_pieces + 2]
    keeps, sends = refs[n_pieces + 2 : n_pieces + 2 + rs], refs[n_pieces + 2 + rs : -2]
    resid, back = refs[-2:]
    z, r, here = lax.axis_index("col"), lax.axis_index("row"), lax.axis_index("help")
    _, rows, span, width = pieces[0].shape
    columns = second.shape[0]
    terms = second.shape[1] // (2 * rows)
    row_index = lax.broadcasted_iota(jnp.int32, (terms, width), 0)
    for i in range(rows):
        for piece, (z_offsets, h_offset) in zip(pieces, spots):
            for e, offset in enumerate(z_offsets):
                spot = (z ^ offset) * helps + (here ^ h_offset)
                resid[i, pl.ds(pl.multiple_of(spot * span, span), span), :] = piece[e, i]
        value = resid[i]
        turned = turn(value.astype(F32), 1.0, -1.0).astype(BF16)
        left = jnp.concatenate([basis[0, i], basis[1, i]], 1)
        out = jnp.dot(left, jnp.concatenate([value, turned], 0), preferred_element_type=F32)
        for j in range(columns):
            left = ranks[i, j] - here * terms
            part = out[j * terms : (j + 1) * terms]
            back[j, i * terms : (i + 1) * terms, :] = jnp.where(row_index < left, part, 0.0)
    quarter = keeps[0].shape[2]

    def keep(d, j, value):
        keeps[d][j] = value

    parts = (len(sends) - 1) // (rs - 1)

    def send(d, j, value):
        refs = sends[:1] if d == 0 else sends[1 + (d - 1) * parts : 1 + d * parts]
        n = refs[0].shape[0]
        refs[j // n][j % n] = value.astype(BF16)

    half = back.shape[1]
    for j in range(columns):
        real = back[j].astype(BF16).T
        turned = jnp.concatenate([-real[width // 2 :], real[: width // 2]], 0)

        def product(right):
            out = jnp.dot(real, right[:half], preferred_element_type=F32)
            return out + jnp.dot(turned, right[half:], preferred_element_type=F32)

        if quarter % LANES == 0:
            for put, h in ((keep, here), (send, 1 - here)):
                places = [((r ^ d) * helps + h) * quarter for d in range(rs)]
                places = [pl.multiple_of(at, quarter) for at in places]
                out = product(jnp.concatenate([second[j, :, pl.ds(at, quarter)] for at in places], 1))
                for d in range(rs):
                    put(d, j, out[:, d * quarter : (d + 1) * quarter])
        else:
            out = product(second[j])
            for n in range(rs):
                for h in range(helps):
                    part = out[:, (n * helps + h) * quarter : (n * helps + h + 1) * quarter]
                    for d in range(rs):
                        pl.when((here == h) & (n ^ r == d))(functools.partial(keep, d, j, part))
                        pl.when((here != h) & (n ^ r == d))(functools.partial(send, d, j, part))


def body(wavefield, basis_factor, second_factor, tile_ranks, observed, amplitude):
    _, columns, quarter, rhs = wavefield.shape
    _, rows, _, terms, tile = basis_factor.shape
    span = observed.shape[2]
    zs, rs, helps = lax.axis_size("col"), lax.axis_size("row"), lax.axis_size("help")
    width = 2 * rhs // CHUNKS
    bits = zs.bit_length() - 1
    far = zs // 2
    near = [1 << b for b in range(bits - 1)]
    z_offsets = [int(format(n, f"0{bits}b")[::-1], 2) for n in range(zs)]

    def share(pieces):
        return pieces + [swap("help", d, m) for d in range(1, helps) for m in pieces]

    first = 5 * columns // 8
    shapes = [((n, quarter, width), BF16) for n in (first, columns - first, columns)]
    waves = call(
        first_kernel,
        "first_waves",
        shapes[:1],
        [in_hbm(wavefield)],
        in_specs=[HBM],
        scratch=[pltpu.VMEM((2, first, quarter, rhs), BF16), pltpu.SemaphoreType.DMA((2,))],
    )
    data = call(
        data_kernel,
        "join_data",
        [((3, rows, span, rhs), BF16)],
        [after(in_hbm(observed), *waves), in_hbm(amplitude)],
        in_specs=[HBM] * 2,
        scratch=[pltpu.SemaphoreType.DMA((2,))],
        cost=LARGE,
    )[0]
    data = [data, swap("col", far, data)]
    rest, whole, *others = call(
        waves_kernel,
        "other_waves",
        shapes[1:] + shapes[2:] * (CHUNKS - 1),
        [after(wavefield, data[0])],
        cost=LARGE,
    )
    waves = [[*waves, rest]] + [[w] for w in others]
    gathered = [[[swap("row", d, w) for w in ws] for d in range(1, rs)] for ws in waves]
    wholes = [whole, *others]

    second, basis = call(
        load_kernel,
        "load_factors",
        [((columns, 2 * rows, terms, tile), BF16), ((2, rows, columns, terms, tile), BF16)],
        [second_factor, basis_factor],
        in_specs=[HBM] * 2,
        scratch=[pltpu.SemaphoreType.DMA((2, 2 * rows))],
        cost=LARGE,
    )
    second = second.reshape(columns, 2 * rows * terms, tile)
    basis = basis.reshape(2, rows, columns * terms, tile)

    def forward(c, mine):
        split = zs if c else SPLIT
        shape, piece = (zs, rows, span, width), (zs // split, rows, span, width)
        pieces = [m for slot in mine for m in slot]
        return call(
            functools.partial(forward_kernel, rs, helps, z_offsets, [len(slot) for slot in mine]),
            "forward_product",
            [(shape, F32)] + [(piece, BF16)] * split,
            [tile_ranks, *pieces, second, basis],
            in_specs=[SM] + [VM] * (len(pieces) + 2),
            scratch=[
                pltpu.VMEM((columns, tile, width), BF16),
                pltpu.VMEM((rows, columns * terms, width), F32),
                pltpu.VMEM((rows, tile, width), F32),
            ],
            limit=16 * MIB,
            cost=LARGE if c else 1,
        )

    def backward(c, pieces, spots):
        whole = (columns, width, quarter)
        parts = 2
        piece = (columns // parts, width, quarter)
        outs = call(
            functools.partial(adjoint_kernel, rs, helps, spots),
            "adjoint_product",
            [(whole, F32)] * rs + [(whole, BF16)] + [(piece, BF16)] * ((rs - 1) * parts),
            [tile_ranks, *pieces, basis, second],
            in_specs=[SM] + [VM] * (len(pieces) + 2),
            scratch=[
                pltpu.VMEM((rows, tile, width), BF16),
                pltpu.VMEM((columns, rows * terms, width), F32),
            ],
            limit=16 * MIB,
            cost=1,
        )
        sends = outs[rs:]
        return outs[:rs], [sends[:1]] + [sends[1 + d * parts : 1 + (d + 1) * parts] for d in range(rs - 1)]

    halved, mirrored, residuals, sent, totals = [], [], [], [], []

    def front(c):
        earlier = [(mirrored[-1][1],)] if c else [(second,), (second, data[1])]
        far_pieces = [[after(m, *e) for m, e in zip(slot, earlier)] for slot in gathered[c]]
        mine = [waves[c]] + far_pieces
        for d in range(1, helps):
            mine.append([swap("help", d, wholes[c])])
            mine.extend([swap("help", d, m) for m in slot] for slot in far_pieces)
        mine = [list(slot) for slot in mine]
        if c:
            mine[0][0] = after(mine[0][0], mirrored[-1][1])
        keep, *sends = forward(c, mine)
        others = [swap("help", 1, send) for send in sends]
        for d in near:
            shape = (keep.shape[0] // 2, rows, span, width)
            keep, send = call(
                halve_kernel, "halve", [(shape, F32), (shape, BF16)], [keep, *others], cost=1
            )
            others = [swap("col", d, send)]
        halved.append(send)
        if c:
            residual_of(c - 1, send)
            keep = after(keep, *residuals[c - 1])
        mirrored.append(call(mirror_kernel, "mirror", [(shape, F32), (shape, BF16)], [keep, *others]))

    def residual_of(c, *earlier):
        keep, send = mirrored[c]
        b = BLOCKS[c > 0]
        residuals.append(
            call(
                functools.partial(residual_kernel, c),
                "residual",
                [((b, rows, span, width), BF16)] * (2 // b),
                [after(keep, *earlier), swap("col", far, send), *data],
                cost=LARGE,
            )
        )

    def rear(c):
        pieces = list(residuals[c])
        offsets = [[0], [far]] if len(pieces) == 2 else [[0, far]]
        own = len(pieces)
        for d in reversed(near):
            pieces = pieces + [swap("col", d, m) for m in pieces]
            offsets = offsets + [[o ^ d for o in os] for os in offsets]
        last = c + 1 == CHUNKS
        earlier = sent if last else [mirrored[c + 1][1]]
        pieces[own:] = [after(m, *earlier) for m in pieces[own:]]
        pieces = share(pieces)
        spots = [(o, e) for e in range(helps) for o in offsets]
        if not last:
            pieces[0] = after(pieces[0], mirrored[c + 1][1])
        keeps, sends = backward(c, pieces, spots)
        if not last:
            residual_of(c + 1, sends[-1][-1])
            keeps = [keeps[0]] + [after(k, *residuals[c + 1]) for k in keeps[1:]]
        shape = (columns, width, quarter)
        shared = [
            call(
                share_kernel,
                "adjoint_share",
                [(shape, BF16)],
                [k, *[swap("help", 1, m) for m in s]],
            )[0]
            for k, s in zip(keeps[1:], sends[1:])
        ]
        if last:
            totals[-1][0] = after(totals[-1][0], *shared)
            totals[-1] = call(total_kernel, "total", [(shape, F32)], totals[-1], cost=LARGE)
        else:
            sent.extend(shared)
        totals.append(
            [keeps[0], swap("help", 1, after(sends[0][0], *shared))]
            + [swap("row", d + 1, m) for d, m in enumerate(shared)]
        )

    for c in range(CHUNKS):
        front(c)
    for c in range(CHUNKS):
        rear(c)

    residual = call(join_kernel, "join", [(observed.shape, BF16)], [r[0] for r in residuals], cost=1)[0]
    adjoint = call(
        final_kernel, "adjoint_sum", [(wavefield.shape, BF16)], [*totals[0], *totals[1]]
    )[0]
    return residual, adjoint


def solution(mesh):
    return jax.shard_map(
        body,
        mesh=mesh,
        in_specs=(
            P("freq", "col", ("row", "help"), None),
            P("freq", "row", "col", "help", None),
            P("freq", "row", "col", "help", None),
            P(("freq", "row"), "col"),
            P("freq", "row", ("col", "help"), None),
            P(("freq", "row"), ("col", "help"), None),
        ),
        out_specs=(
            P("freq", "row", ("col", "help"), None),
            P("freq", "col", ("row", "help"), None),
        ),
        check_vma=False,
    )
```

```python
import functools

import jax
import jax.numpy as jnp
from jax import lax
from jax.experimental import pallas as pl
from jax.experimental.pallas import tpu as pltpu
from jax.sharding import PartitionSpec as P

BF16 = jnp.bfloat16
F32 = jnp.float32
CHUNKS = 2
LANES = 128
VM = pl.BlockSpec(memory_space=pltpu.VMEM)
SM = pl.BlockSpec(memory_space=pltpu.SMEM)
HBM = pl.BlockSpec(memory_space=pltpu.HBM)
ANY = pl.BlockSpec(memory_space=pl.ANY)
MIB = 1024 * 1024
LARGE = 10**10
SPLIT = 2
HEAD = 1
OWN = 1


def call(kernel, name, outs, ins, in_specs=None, out_specs=None, scratch=(), limit=6 * MIB, cost=10**6):
    return pl.pallas_call(
        kernel,
        out_shape=[jax.ShapeDtypeStruct(shape, kind) for shape, kind in outs],
        in_specs=in_specs or [VM] * len(ins),
        out_specs=out_specs or [VM] * len(outs),
        scratch_shapes=list(scratch),
        compiler_params=pltpu.CompilerParams(vmem_limit_bytes=limit),
        cost_estimate=pl.CostEstimate(flops=cost, bytes_accessed=10**4, transcendentals=0),
        name=name,
    )(*ins)


def in_hbm(value):
    return pltpu.with_memory_space_constraint(value, pltpu.HBM)


def swap(axis_name, step, value):
    size = lax.axis_size(axis_name)
    return lax.ppermute(value, axis_name, [(i, i ^ step) for i in range(size)])


def after(value, *earlier):
    return lax.optimization_barrier((value, *earlier))[0]


def turn(value, first, second):
    width = value.shape[-1]
    lane = lax.broadcasted_iota(jnp.int32, value.shape, value.ndim - 1)
    sign = jnp.where(lane < width // 2, first, second).astype(F32)
    return pltpu.roll(value, width // 2, value.ndim - 1) * sign


def side_by_side(source, j, c, part):
    lanes = slice(c * part, (c + 1) * part)
    return jnp.concatenate([source[0, j, :, lanes], source[1, j, :, lanes]], -1)


def first_kernel(source, observed, amplitude, out, data, held, sems):
    n = out.shape[0]
    copies = [pltpu.make_async_copy(source.at[p, :n], held.at[p], sems.at[p]) for p in range(2)]
    copies.append(pltpu.make_async_copy(observed, data.at[:2], sems.at[2]))
    copies.append(pltpu.make_async_copy(amplitude, data.at[2], sems.at[3]))
    for copy in copies:
        copy.start()
    for copy in copies[:2]:
        copy.wait()
    for j in range(n):
        out[j] = side_by_side(held, j, 0, out.shape[-1] // 2)
    for copy in copies[2:]:
        copy.wait()


def relay_kernel(source, out):
    out[...] = source[...]


def waves_kernel(source, rest, whole, *others):
    columns, part = whole.shape[0], whole.shape[-1] // 2
    first = columns - rest.shape[0]
    for j in range(columns):
        whole[j] = side_by_side(source, j, 0, part)
        if j >= first:
            rest[j - first] = whole[j]
        for c, other in enumerate(others):
            other[j] = side_by_side(source, j, c + 1, part)


def load_kernel(second_in, basis_in, second, basis, sems):
    rows = second_in.shape[1]
    copies = []
    for p in range(2):
        for i in range(rows):
            n = p * rows + i
            copies.append(pltpu.make_async_copy(second_in.at[p, i], second.at[:, n], sems.at[0, n]))
            copies.append(pltpu.make_async_copy(basis_in.at[p, i], basis.at[p, i], sems.at[1, n]))
    for copy in copies:
        copy.start()
    for copy in copies:
        copy.wait()


def halve_kernel(mine, *refs):
    others, keep, send = refs[:-2], refs[-2], refs[-1]
    n = keep.shape[0]
    total = jnp.concatenate([other[...] for other in others], 0).astype(F32) + mine[...]
    keep[...] = total[:n]
    send[...] = total[n:].astype(BF16)


def mirror_kernel(mine, *refs):
    others, keep, send = refs[:-2], refs[-2], refs[-1]
    total = jnp.concatenate([other[...] for other in others], 0).astype(F32) + mine[...]
    keep[...] = total
    n = keep.shape[0]
    for e in range(n):
        send[e] = total[n - 1 - e].astype(BF16)


def residual_kernel(c, mine, other, *refs):
    arrays, out = refs[:2], refs[2]
    part = out.shape[-1] // 2
    lanes = slice(c * part, (c + 1) * part)
    for e in range(2):
        total = mine[e] + other[e].astype(F32)
        data = jnp.concatenate([arrays[e][p, :, :, lanes] for p in range(2)], -1)
        weight = jnp.concatenate([arrays[e][2, :, :, lanes]] * 2, -1)
        value = (weight.astype(F32) * (total - data.astype(F32))).astype(BF16)
        out[e] = value


def spread_kernel(source, *outs):
    for e, out in enumerate(outs):
        out[0] = source[e]


def join_kernel(*refs):
    out = refs[-1]
    part = out.shape[-1] // (len(refs) - 1)
    for p in range(2):
        out[p] = jnp.concatenate([ref[0, :, :, p * part : (p + 1) * part] for ref in refs[:-1]], -1)


def share_kernel(mine, *refs):
    others, out = refs[:-1], refs[-1]
    n = others[0].shape[0]
    for k, other in enumerate(others):
        at = slice(k * n, (k + 1) * n)
        out[at] = (mine[at] + other[...].astype(F32)).astype(BF16)


def total_kernel(mine, *refs):
    others, out = refs[:-1], refs[-1]
    total = mine[...]
    for ref in others:
        total = total + ref[...].astype(F32)
    out[...] = total


def final_kernel(done, mine, *refs):
    *others, out, out_ref, sems = refs
    part = mine.shape[1] // 2
    columns = out_ref.shape[1]
    copies = []
    for j in range(columns):
        for p in range(2):
            lanes = slice(p * part, (p + 1) * part)
            total = mine[j, lanes, :]
            for ref in others:
                total = total + ref[j, lanes, :].astype(F32)
            out_ref[p, j] = jnp.concatenate([done[j, lanes, :], total], 0).astype(out_ref.dtype).T
        n = len(copies)
        if j + 1 == (n + 1) * columns // sems.shape[0]:
            at = slice(n * columns // sems.shape[0], j + 1)
            copies.append(pltpu.make_async_copy(out_ref.at[:, at], out.at[:, at], sems.at[n]))
            copies[-1].start()
    for copy in copies:
        copy.wait()


def slots_of(counts, refs):
    slots, at = [], 0
    for count in counts:
        slots.append([(ref, j) for ref in refs[at : at + count] for j in range(ref.shape[0])])
        at += count
    return slots, refs[at:]


def products(slots, places, columns, second, waves):
    _, quarter, width = slots[0][0][0].shape
    half = second.shape[1] // 2
    at_all = [pl.multiple_of(at * quarter, quarter) for at in places]
    for n, j in enumerate(columns):
        parts = [ref[k] for ref, k in (slot[n if len(slot) == len(columns) else j] for slot in slots)]
        if quarter % LANES == 0:
            left = jnp.concatenate([second[j, :, pl.ds(at, quarter)] for at in at_all], 1)
            right = jnp.concatenate(parts, 0)
        else:
            waves[n] = jnp.zeros(waves.shape[1:], BF16)
            for at, part in zip(at_all, parts):
                waves[n, pl.ds(at, quarter), :] = part
            left, right = second[j], waves[n]
        out = jnp.dot(left, right, preferred_element_type=F32)
        yield n, j, out[:half] + turn(out[half:], 1.0, -1.0)


def near_kernel(second, *refs):
    r, here = lax.axis_index("row"), lax.axis_index("help")
    helps = lax.axis_size("help")
    *refs, waves = refs
    parts = len(refs) // (helps + 1)
    for c in range(parts):
        out = refs[parts * helps + c]
        slots = [[(ref, j) for j in range(ref.shape[0])] for ref in refs[c * helps : (c + 1) * helps]]
        places = [r * helps + (here ^ d) for d in range(helps)]
        rows = out.shape[0]
        for n, j, value in products(slots, places, range(second.shape[0]), second, waves):
            terms = value.shape[0] // rows
            for i in range(rows):
                out[i, j * terms : (j + 1) * terms, :] = value[i * terms : (i + 1) * terms]


def coefficients(slots, columns, ranks, second, near, waves, coef):
    rs, helps = lax.axis_size("row"), lax.axis_size("help")
    r, here = lax.axis_index("row"), lax.axis_index("help")
    rows = coef.shape[0]
    terms = second.shape[1] // (2 * rows)
    row_index = lax.broadcasted_iota(jnp.int32, (terms, coef.shape[2]), 0)
    places = [(r ^ d) * helps + (here ^ e) for e in range(helps) for d in range(1, rs)]
    for n, j, value in products(slots, places, columns, second, waves):
        for i in range(rows):
            left = ranks[i, j] - here * terms
            part = value[i * terms : (i + 1) * terms] + near[i, j * terms : (j + 1) * terms, :]
            coef[i, n * terms : (n + 1) * terms, :] = jnp.where(row_index < left, part, 0.0)


def head_kernel(counts, ranks, *refs):
    slots, (second, near, coef, waves) = slots_of(counts, refs)
    coefficients(slots, range(len(slots[0])), ranks, second, near, waves, coef)


def forward_kernel(z_offsets, counts, n_heads, ranks, *refs):
    slots, refs = slots_of(counts, refs)
    (second, basis, near), heads, refs = refs[:3], refs[3 : 3 + n_heads], refs[3 + n_heads :]
    keep_out, *sends, waves, coef, fwd = refs
    n_send = sends[0].shape[0]
    helps = lax.axis_size("help")
    z, here = lax.axis_index("col"), lax.axis_index("help")
    columns = second.shape[0]
    coefficients(slots, range(columns - len(slots[0]), columns), ranks, second, near, waves, coef)
    rows = basis.shape[1]
    _, _, span, _ = keep_out.shape
    dims = (((0,), (0,)), ((), ()))
    for i in range(rows):
        value = jnp.concatenate([head[i] for head in heads] + [coef[i]], 0)
        left = jnp.concatenate([value, turn(value, -1.0, 1.0)], 0).astype(BF16)
        right = jnp.concatenate([basis[0, i], basis[1, i]], 0)
        out = lax.dot_general(left, right, dims, preferred_element_type=F32)
        fwd[i] = out.T
        for n, offset in enumerate(z_offsets):
            block = (z ^ offset) * helps
            at = pl.multiple_of((block + here) * span, span)
            keep_out[n, i] = fwd[i, pl.ds(at, span), :].astype(keep_out.dtype)
            at = pl.multiple_of((block + 1 - here) * span, span)
            sends[n // n_send][n % n_send, i] = fwd[i, pl.ds(at, span), :].astype(BF16)


def adjoint_terms(offsets, back, second, keeps, sends):
    rs, helps = lax.axis_size("row"), lax.axis_size("help")
    r, here = lax.axis_index("row"), lax.axis_index("help")
    _, width, quarter = keeps[0].shape
    parts = len(sends) // len(offsets)
    half = back.shape[1]

    def keep(d, j, value):
        keeps[d][j] = value

    def send(d, j, value):
        refs = sends[d * parts : (d + 1) * parts]
        n = refs[0].shape[0]
        refs[j // n][j % n] = value.astype(BF16)

    for j in range(back.shape[0]):
        real = back[j].astype(BF16).T
        turned = jnp.concatenate([-real[width // 2 :], real[: width // 2]], 0)

        def product(right):
            out = jnp.dot(real, right[:half], preferred_element_type=F32)
            return out + jnp.dot(turned, right[half:], preferred_element_type=F32)

        if quarter % LANES == 0:
            for n, d in enumerate(offsets):
                places = [((r ^ d) * helps + h) * quarter for h in (here, 1 - here)]
                places = [pl.multiple_of(at, quarter) for at in places]
                out = product(jnp.concatenate([second[j, :, pl.ds(at, quarter)] for at in places], 1))
                keep(n, j, out[:, :quarter])
                send(n, j, out[:, quarter:])
        else:
            out = product(second[j])
            for m in range(rs):
                for h in range(helps):
                    part = out[:, (m * helps + h) * quarter : (m * helps + h + 1) * quarter]
                    for n, d in enumerate(offsets):
                        pl.when((here == h) & (m ^ r == d))(functools.partial(keep, n, j, part))
                        pl.when((here != h) & (m ^ r == d))(functools.partial(send, n, j, part))


def adjoint_kernel(offsets, spots, ranks, *refs):
    n_pieces, n = len(spots), len(offsets)
    pieces, (basis, second), refs = refs[:n_pieces], refs[n_pieces : n_pieces + 2], refs[n_pieces + 2 :]
    back_out, keeps, sends, (resid, back) = refs[0], refs[1 : 1 + n], refs[1 + n : -2], refs[-2:]
    helps = lax.axis_size("help")
    z, here = lax.axis_index("col"), lax.axis_index("help")
    _, rows, span, width = pieces[0].shape
    columns = second.shape[0]
    terms = second.shape[1] // (2 * rows)
    row_index = lax.broadcasted_iota(jnp.int32, (terms, width), 0)
    for i in range(rows):
        for piece, (z_offsets, h_offset) in zip(pieces, spots):
            for e, offset in enumerate(z_offsets):
                spot = (z ^ offset) * helps + (here ^ h_offset)
                resid[i, pl.ds(pl.multiple_of(spot * span, span), span), :] = piece[e, i]
        value = resid[i]
        turned = turn(value.astype(F32), 1.0, -1.0).astype(BF16)
        left = jnp.concatenate([basis[0, i], basis[1, i]], 1)
        out = jnp.dot(left, jnp.concatenate([value, turned], 0), preferred_element_type=F32)
        for j in range(columns):
            left = ranks[i, j] - here * terms
            part = out[j * terms : (j + 1) * terms]
            back[j, i * terms : (i + 1) * terms, :] = jnp.where(row_index < left, part, 0.0)
    back_out[...] = back[...].astype(BF16)
    adjoint_terms(offsets, back, second, keeps, sends)


def own_kernel(back, second, keep, send):
    adjoint_terms([0], back, second, [keep], [send])


def body(wavefield, basis_factor, second_factor, tile_ranks, observed, amplitude):
    _, columns, quarter, rhs = wavefield.shape
    _, rows, _, terms, tile = basis_factor.shape
    span = observed.shape[2]
    zs, rs, helps = lax.axis_size("col"), lax.axis_size("row"), lax.axis_size("help")
    width = 2 * rhs // CHUNKS
    bits = zs.bit_length() - 1
    far = zs // 2
    near = [1 << b for b in range(bits - 1)]
    z_offsets = [int(format(n, f"0{bits}b")[::-1], 2) for n in range(zs)]

    def share(pieces):
        return pieces + [swap("help", d, m) for d in range(1, helps) for m in pieces]

    first = 5 * columns // 8
    shapes = [((n, quarter, width), BF16) for n in (first, columns - first, columns)]
    head, data = call(
        first_kernel,
        "first_waves",
        shapes[:1] + [((3, rows, span, rhs), BF16)],
        [in_hbm(wavefield), in_hbm(observed), in_hbm(amplitude)],
        in_specs=[HBM] * 3,
        scratch=[pltpu.VMEM((2, first, quarter, rhs), BF16), pltpu.SemaphoreType.DMA((4,))],
    )
    data = call(relay_kernel, "relay_data", [(data.shape, BF16)], [after(data, head)], cost=LARGE)[0]
    data = [data, swap("col", far, data)]
    rest, whole, *others = call(
        waves_kernel,
        "other_waves",
        shapes[1:] + shapes[2:] * (CHUNKS - 1),
        [after(wavefield, data[0])],
        cost=LARGE,
    )
    waves = [[head, rest]] + [[w] for w in others]
    gathered = [[[swap("row", d, w) for w in ws] for d in range(1, rs)] for ws in waves]
    wholes = [whole, *others]

    second, basis = call(
        load_kernel,
        "load_factors",
        [((columns, 2 * rows, terms, tile), BF16), ((2, rows, columns, terms, tile), BF16)],
        [second_factor, basis_factor],
        in_specs=[HBM] * 2,
        scratch=[pltpu.SemaphoreType.DMA((2, 2 * rows))],
        cost=LARGE,
    )
    second = second.reshape(columns, 2 * rows * terms, tile)
    basis = basis.reshape(2, rows, columns * terms, tile)
    nears = call(
        near_kernel,
        "near_products",
        [((rows, columns * terms, width), F32)] * CHUNKS,
        [second, *[m for w in wholes for m in share([w])]],
        scratch=[pltpu.VMEM((columns, tile, width), BF16)],
        limit=16 * MIB,
        cost=1,
    )

    def forward(c, mine, heads):
        split = zs if c else SPLIT
        shape, piece = (zs, rows, span, width), (zs // split, rows, span, width)
        pieces = [m for slot in mine for m in slot]
        n = sum(m.shape[0] for m in mine[0])
        return call(
            functools.partial(forward_kernel, z_offsets, [len(slot) for slot in mine], len(heads)),
            "forward_product",
            [(shape, F32)] + [(piece, BF16)] * split,
            [tile_ranks, *pieces, second, basis, nears[c], *heads],
            in_specs=[SM] + [VM] * (len(pieces) + 3 + len(heads)),
            scratch=[
                pltpu.VMEM((n, tile, width), BF16),
                pltpu.VMEM((rows, n * terms, width), F32),
                pltpu.VMEM((rows, tile, width), F32),
            ],
            limit=16 * MIB,
            cost=LARGE if c else 1,
        )

    def backward(c, pieces, spots):
        whole, parts = (columns, width, quarter), 2
        piece = (columns // parts, width, quarter)
        back, *outs = call(
            functools.partial(adjoint_kernel, list(range(1, rs)), spots),
            "adjoint_product",
            [((columns, rows * terms, width), BF16)]
            + [(whole, F32)] * (rs - 1)
            + [(piece, BF16)] * ((rs - 1) * parts),
            [tile_ranks, *pieces, basis, second],
            in_specs=[SM] + [VM] * (len(pieces) + 2),
            scratch=[
                pltpu.VMEM((rows, tile, width), BF16),
                pltpu.VMEM((columns, rows * terms, width), F32),
            ],
            limit=16 * MIB,
            cost=1,
        )
        keeps, sends = outs[: rs - 1], outs[rs - 1 :]
        own = call(
            own_kernel, "own_quarter", [(whole, F32), (whole, BF16)], [back, second], limit=16 * MIB, cost=OWN
        )
        return [own[0], *keeps], [own[1:]] + [sends[d * parts : (d + 1) * parts] for d in range(rs - 1)]

    halved, mirrored, residuals, sent, totals, joined = [], [], [], [], [], []

    def front(c):
        earlier = [(mirrored[-1][1],)] if c else [(second, *nears), (second, data[1])]
        far_pieces = [[after(m, *e) for m, e in zip(slot, earlier)] for slot in gathered[c]]
        mine = list(far_pieces)
        for d in range(1, helps):
            mine.extend([swap("help", d, m) for m in slot] for slot in far_pieces)
        heads = []
        if c:
            mine[0][0] = after(mine[0][0], mirrored[-1][1])
        else:
            pieces = [slot[0] for slot in mine]
            heads = call(
                functools.partial(head_kernel, [1] * len(pieces)),
                "first_coefficients",
                [((rows, first * terms, width), F32)],
                [tile_ranks, *pieces, second, nears[0]],
                in_specs=[SM] + [VM] * (len(pieces) + 2),
                scratch=[pltpu.VMEM((first, tile, width), BF16)],
                limit=16 * MIB,
                cost=HEAD,
            )
            mine = [slot[1:] or slot for slot in mine]
        keep, *sends = forward(c, mine, heads)
        others = [swap("help", 1, send) for send in sends]
        for d in near:
            shape = (keep.shape[0] // 2, rows, span, width)
            keep, send = call(
                halve_kernel, "halve", [(shape, F32), (shape, BF16)], [keep, *others], cost=1
            )
            others = [swap("col", d, send)]
        halved.append(send)
        if c:
            residual_of(c - 1, send)
            keep = after(keep, *residuals[c - 1])
        mirrored.append(call(mirror_kernel, "mirror", [(shape, F32), (shape, BF16)], [keep, *others]))

    def residual_of(c, *earlier):
        keep, send = mirrored[c]
        residuals.append(
            call(
                functools.partial(residual_kernel, c),
                "residual",
                [((2, rows, span, width), BF16)],
                [after(keep, *earlier), swap("col", far, send), *data],
                cost=LARGE,
            )
        )

    def rear(c):
        pieces, offsets = list(residuals[c]), [[0, far]]
        for d in reversed(near):
            pieces = pieces + [swap("col", d, m) for m in pieces]
            offsets = offsets + [[o ^ d for o in os] for os in offsets]
        last = c + 1 == CHUNKS
        earlier = sent if last else [mirrored[c + 1][1]]
        pieces[1:] = [after(m, *earlier) for m in pieces[1:]]
        passed = list(pieces)
        if not last:
            block = ((1, rows, span, width), BF16)
            for m in pieces[1:]:
                passed.extend(call(spread_kernel, "spread", [block] * 2, [m], cost=1))
            passed[1 : len(pieces)] = []
            passed_offsets = offsets[:1] + [[o] for os in offsets[1:] for o in os]
        else:
            passed_offsets = offsets
        pieces = pieces + [swap("help", d, m) for d in range(1, helps) for m in passed]
        spots = [(o, 0) for o in offsets] + [(o, e) for e in range(1, helps) for o in passed_offsets]
        if not last:
            pieces[0] = after(pieces[0], mirrored[c + 1][1])
        else:
            joined.extend(call(join_kernel, "join", [(observed.shape, BF16)], [r[0] for r in residuals]))
            pieces[0] = after(pieces[0], *joined)
        keeps, sends = backward(c, pieces, spots)
        if not last:
            residual_of(c + 1, sends[0][0])
            keeps = [keeps[0]] + [after(k, *residuals[c + 1]) for k in keeps[1:]]
        shape = (columns, width, quarter)
        shared = [
            call(
                share_kernel,
                "adjoint_share",
                [(shape, BF16)],
                [k, *[swap("help", 1, m) for m in s]],
            )[0]
            for k, s in zip(keeps[1:], sends[1:])
        ]
        if last:
            totals[-1][0] = after(totals[-1][0], *shared)
            mine, theirs, *others = totals[-1]
            mine = call(total_kernel, "total", [(shape, F32)], [mine, *others], cost=1)[0]
            totals[-1] = call(total_kernel, "total", [(shape, F32)], [mine, theirs], cost=LARGE)
        else:
            sent.extend(shared)
        totals.append(
            [keeps[0], swap("help", 1, after(sends[0][0], *shared))]
            + [swap("row", d + 1, m) for d, m in enumerate(shared)]
        )

    for c in range(CHUNKS):
        front(c)
    for c in range(CHUNKS):
        rear(c)

    adjoint = call(
        final_kernel,
        "adjoint_sum",
        [(wavefield.shape, BF16)],
        [*totals[0], *totals[1]],
        out_specs=[HBM],
        scratch=[pltpu.VMEM(wavefield.shape, BF16), pltpu.SemaphoreType.DMA((4,))],
    )[0]
    return joined[0], adjoint


def solution(mesh):
    return jax.shard_map(
        body,
        mesh=mesh,
        in_specs=(
            P("freq", "col", ("row", "help"), None),
            P("freq", "row", "col", "help", None),
            P("freq", "row", "col", "help", None),
            P(("freq", "row"), "col"),
            P("freq", "row", ("col", "help"), None),
            P(("freq", "row"), ("col", "help"), None),
        ),
        out_specs=(
            P("freq", "row", ("col", "help"), None),
            P("freq", "col", ("row", "help"), None),
        ),
        check_vma=False,
    )
```

```python
import functools

import jax
import jax.numpy as jnp
from jax import lax
from jax.experimental import pallas as pl
from jax.experimental.pallas import tpu as pltpu
from jax.sharding import PartitionSpec as P

BF16 = jnp.bfloat16
F32 = jnp.float32
CHUNKS = 2
LANES = 128
VM = pl.BlockSpec(memory_space=pltpu.VMEM)
SM = pl.BlockSpec(memory_space=pltpu.SMEM)
HBM = pl.BlockSpec(memory_space=pltpu.HBM)
ANY = pl.BlockSpec(memory_space=pl.ANY)
MIB = 1024 * 1024
LARGE = 10**10
SPLIT = 2
HEAD = 1
OWN = 1


def call(kernel, name, outs, ins, in_specs=None, out_specs=None, scratch=(), limit=6 * MIB, cost=10**6):
    return pl.pallas_call(
        kernel,
        out_shape=[jax.ShapeDtypeStruct(shape, kind) for shape, kind in outs],
        in_specs=in_specs or [VM] * len(ins),
        out_specs=out_specs or [VM] * len(outs),
        scratch_shapes=list(scratch),
        compiler_params=pltpu.CompilerParams(vmem_limit_bytes=limit),
        cost_estimate=pl.CostEstimate(flops=cost, bytes_accessed=10**4, transcendentals=0),
        name=name,
    )(*ins)


def in_hbm(value):
    return pltpu.with_memory_space_constraint(value, pltpu.HBM)


def swap(axis_name, step, value):
    size = lax.axis_size(axis_name)
    return lax.ppermute(value, axis_name, [(i, i ^ step) for i in range(size)])


def after(value, *earlier):
    return lax.optimization_barrier((value, *earlier))[0]


def turn(value, first, second):
    width = value.shape[-1]
    lane = lax.broadcasted_iota(jnp.int32, value.shape, value.ndim - 1)
    sign = jnp.where(lane < width // 2, first, second).astype(F32)
    return pltpu.roll(value, width // 2, value.ndim - 1) * sign


def side_by_side(source, j, c, part):
    lanes = slice(c * part, (c + 1) * part)
    return jnp.concatenate([source[0, j, :, lanes], source[1, j, :, lanes]], -1)


def first_kernel(source, observed, amplitude, out, data, held, sems):
    n = out.shape[0]
    copies = [pltpu.make_async_copy(source.at[p, :n], held.at[p], sems.at[p]) for p in range(2)]
    copies.append(pltpu.make_async_copy(observed, data.at[:2], sems.at[2]))
    copies.append(pltpu.make_async_copy(amplitude, data.at[2], sems.at[3]))
    for copy in copies:
        copy.start()
    for copy in copies[:2]:
        copy.wait()
    for j in range(n):
        out[j] = side_by_side(held, j, 0, out.shape[-1] // 2)
    for copy in copies[2:]:
        copy.wait()


def relay_kernel(source, out):
    out[...] = source[...]


def waves_kernel(source, rest, whole, *others):
    columns, part = whole.shape[0], whole.shape[-1] // 2
    first = columns - rest.shape[0]
    for j in range(columns):
        whole[j] = side_by_side(source, j, 0, part)
        if j >= first:
            rest[j - first] = whole[j]
        for c, other in enumerate(others):
            other[j] = side_by_side(source, j, c + 1, part)


def load_kernel(second_in, basis_in, second, basis, sems):
    rows = second_in.shape[1]
    copies = []
    for p in range(2):
        for i in range(rows):
            n = p * rows + i
            copies.append(pltpu.make_async_copy(second_in.at[p, i], second.at[:, n], sems.at[0, n]))
            copies.append(pltpu.make_async_copy(basis_in.at[p, i], basis.at[p, i], sems.at[1, n]))
    for copy in copies:
        copy.start()
    for copy in copies:
        copy.wait()


def halve_kernel(mine, *refs):
    others, keep, send = refs[:-2], refs[-2], refs[-1]
    n = keep.shape[0]
    total = jnp.concatenate([other[...] for other in others], 0).astype(F32) + mine[...]
    keep[...] = total[:n]
    send[...] = total[n:].astype(BF16)


def sums_kernel(mine, *refs):
    others, send = refs[:-1], refs[-1]
    n = send.shape[0]
    total = jnp.concatenate([other[...] for other in others], 0).astype(F32) + mine[n:]
    send[...] = total.astype(BF16)


def stay_kernel(mine, *refs):
    *others, arrived, keep, send = refs
    n = keep.shape[0]
    total = jnp.concatenate([other[...] for other in others], 0).astype(F32) + mine[:n]
    total = total + arrived[...].astype(F32)
    keep[...] = total
    for e in range(n):
        send[e] = total[n - 1 - e].astype(BF16)


def mirror_kernel(mine, *refs):
    others, keep, send = refs[:-2], refs[-2], refs[-1]
    total = jnp.concatenate([other[...] for other in others], 0).astype(F32) + mine[...]
    keep[...] = total
    n = keep.shape[0]
    for e in range(n):
        send[e] = total[n - 1 - e].astype(BF16)


def residual_kernel(c, mine, other, *refs):
    arrays, out = refs[:2], refs[2]
    part = out.shape[-1] // 2
    lanes = slice(c * part, (c + 1) * part)
    for e in range(2):
        total = mine[e] + other[e].astype(F32)
        data = jnp.concatenate([arrays[e][p, :, :, lanes] for p in range(2)], -1)
        weight = jnp.concatenate([arrays[e][2, :, :, lanes]] * 2, -1)
        value = (weight.astype(F32) * (total - data.astype(F32))).astype(BF16)
        out[e] = value


def spread_kernel(source, *outs):
    for e, out in enumerate(outs):
        out[0] = source[e]


def join_kernel(*refs):
    out = refs[-1]
    part = out.shape[-1] // (len(refs) - 1)
    for p in range(2):
        out[p] = jnp.concatenate([ref[0, :, :, p * part : (p + 1) * part] for ref in refs[:-1]], -1)


def share_kernel(mine, *refs):
    others, out = refs[:-1], refs[-1]
    n = others[0].shape[0]
    for k, other in enumerate(others):
        at = slice(k * n, (k + 1) * n)
        out[at] = (mine[at] + other[...].astype(F32)).astype(BF16)


def total_kernel(mine, *refs):
    others, out = refs[:-1], refs[-1]
    total = mine[...]
    for ref in others:
        total = total + ref[...].astype(F32)
    out[...] = total


def final_kernel(done, mine, *refs):
    *others, out, out_ref, sems = refs
    part = mine.shape[1] // 2
    columns = out_ref.shape[1]
    copies = []
    for j in range(columns):
        for p in range(2):
            lanes = slice(p * part, (p + 1) * part)
            total = mine[j, lanes, :]
            for ref in others:
                total = total + ref[j, lanes, :].astype(F32)
            out_ref[p, j] = jnp.concatenate([done[j, lanes, :], total], 0).astype(out_ref.dtype).T
        n = len(copies)
        if j + 1 == (n + 1) * columns // sems.shape[0]:
            at = slice(n * columns // sems.shape[0], j + 1)
            copies.append(pltpu.make_async_copy(out_ref.at[:, at], out.at[:, at], sems.at[n]))
            copies[-1].start()
    for copy in copies:
        copy.wait()


def slots_of(counts, refs):
    slots, at = [], 0
    for count in counts:
        slots.append([(ref, j) for ref in refs[at : at + count] for j in range(ref.shape[0])])
        at += count
    return slots, refs[at:]


def products(slots, places, columns, second, waves):
    _, quarter, width = slots[0][0][0].shape
    half = second.shape[1] // 2
    at_all = [pl.multiple_of(at * quarter, quarter) for at in places]
    for n, j in enumerate(columns):
        parts = [ref[k] for ref, k in (slot[n if len(slot) == len(columns) else j] for slot in slots)]
        if quarter % LANES == 0:
            left = jnp.concatenate([second[j, :, pl.ds(at, quarter)] for at in at_all], 1)
            right = jnp.concatenate(parts, 0)
        else:
            waves[n] = jnp.zeros(waves.shape[1:], BF16)
            for at, part in zip(at_all, parts):
                waves[n, pl.ds(at, quarter), :] = part
            left, right = second[j], waves[n]
        out = jnp.dot(left, right, preferred_element_type=F32)
        yield n, j, out[:half] + turn(out[half:], 1.0, -1.0)


def near_kernel(second, *refs):
    r, here = lax.axis_index("row"), lax.axis_index("help")
    helps = lax.axis_size("help")
    *refs, waves = refs
    parts = len(refs) // (helps + 1)
    for c in range(parts):
        out = refs[parts * helps + c]
        slots = [[(ref, j) for j in range(ref.shape[0])] for ref in refs[c * helps : (c + 1) * helps]]
        places = [r * helps + (here ^ d) for d in range(helps)]
        rows = out.shape[0]
        for n, j, value in products(slots, places, range(second.shape[0]), second, waves):
            terms = value.shape[0] // rows
            for i in range(rows):
                out[i, j * terms : (j + 1) * terms, :] = value[i * terms : (i + 1) * terms]


def coefficients(slots, columns, ranks, second, near, waves, coef):
    rs, helps = lax.axis_size("row"), lax.axis_size("help")
    r, here = lax.axis_index("row"), lax.axis_index("help")
    rows = coef.shape[0]
    terms = second.shape[1] // (2 * rows)
    row_index = lax.broadcasted_iota(jnp.int32, (terms, coef.shape[2]), 0)
    places = [(r ^ d) * helps + (here ^ e) for e in range(helps) for d in range(1, rs)]
    for n, j, value in products(slots, places, columns, second, waves):
        for i in range(rows):
            left = ranks[i, j] - here * terms
            part = value[i * terms : (i + 1) * terms] + near[i, j * terms : (j + 1) * terms, :]
            coef[i, n * terms : (n + 1) * terms, :] = jnp.where(row_index < left, part, 0.0)


def head_kernel(counts, ranks, *refs):
    slots, (second, near, coef, waves) = slots_of(counts, refs)
    coefficients(slots, range(len(slots[0])), ranks, second, near, waves, coef)


def forward_kernel(z_offsets, counts, n_heads, ranks, *refs):
    slots, refs = slots_of(counts, refs)
    (second, basis, near), heads, refs = refs[:3], refs[3 : 3 + n_heads], refs[3 + n_heads :]
    keep_out, *sends, waves, coef, fwd = refs
    n_send = sends[0].shape[0]
    helps = lax.axis_size("help")
    z, here = lax.axis_index("col"), lax.axis_index("help")
    columns = second.shape[0]
    coefficients(slots, range(columns - len(slots[0]), columns), ranks, second, near, waves, coef)
    rows = basis.shape[1]
    _, _, span, _ = keep_out.shape
    dims = (((0,), (0,)), ((), ()))
    for i in range(rows):
        value = jnp.concatenate([head[i] for head in heads] + [coef[i]], 0)
        left = jnp.concatenate([value, turn(value, -1.0, 1.0)], 0).astype(BF16)
        right = jnp.concatenate([basis[0, i], basis[1, i]], 0)
        out = lax.dot_general(left, right, dims, preferred_element_type=F32)
        fwd[i] = out.T
        for n, offset in enumerate(z_offsets):
            block = (z ^ offset) * helps
            at = pl.multiple_of((block + here) * span, span)
            keep_out[n, i] = fwd[i, pl.ds(at, span), :].astype(keep_out.dtype)
            at = pl.multiple_of((block + 1 - here) * span, span)
            sends[n // n_send][n % n_send, i] = fwd[i, pl.ds(at, span), :].astype(BF16)


def adjoint_terms(offsets, back, second, keeps, sends):
    rs, helps = lax.axis_size("row"), lax.axis_size("help")
    r, here = lax.axis_index("row"), lax.axis_index("help")
    _, width, quarter = keeps[0].shape
    parts = len(sends) // len(offsets)
    half = back.shape[1]

    def keep(d, j, value):
        keeps[d][j] = value

    def send(d, j, value):
        refs = sends[d * parts : (d + 1) * parts]
        n = refs[0].shape[0]
        refs[j // n][j % n] = value.astype(BF16)

    for j in range(back.shape[0]):
        real = back[j].astype(BF16).T
        turned = jnp.concatenate([-real[width // 2 :], real[: width // 2]], 0)

        def product(right):
            out = jnp.dot(real, right[:half], preferred_element_type=F32)
            return out + jnp.dot(turned, right[half:], preferred_element_type=F32)

        if quarter % LANES == 0:
            for n, d in enumerate(offsets):
                places = [((r ^ d) * helps + h) * quarter for h in (here, 1 - here)]
                places = [pl.multiple_of(at, quarter) for at in places]
                out = product(jnp.concatenate([second[j, :, pl.ds(at, quarter)] for at in places], 1))
                keep(n, j, out[:, :quarter])
                send(n, j, out[:, quarter:])
        else:
            out = product(second[j])
            for m in range(rs):
                for h in range(helps):
                    part = out[:, (m * helps + h) * quarter : (m * helps + h + 1) * quarter]
                    for n, d in enumerate(offsets):
                        pl.when((here == h) & (m ^ r == d))(functools.partial(keep, n, j, part))
                        pl.when((here != h) & (m ^ r == d))(functools.partial(send, n, j, part))


def adjoint_kernel(offsets, spots, ranks, *refs):
    n_pieces, n = len(spots), len(offsets)
    pieces, (basis, second), refs = refs[:n_pieces], refs[n_pieces : n_pieces + 2], refs[n_pieces + 2 :]
    back_out, keeps, sends, (resid, back) = refs[0], refs[1 : 1 + n], refs[1 + n : -2], refs[-2:]
    helps = lax.axis_size("help")
    z, here = lax.axis_index("col"), lax.axis_index("help")
    _, rows, span, width = pieces[0].shape
    columns = second.shape[0]
    terms = second.shape[1] // (2 * rows)
    row_index = lax.broadcasted_iota(jnp.int32, (terms, width), 0)
    for i in range(rows):
        for piece, (z_offsets, h_offset) in zip(pieces, spots):
            for e, offset in enumerate(z_offsets):
                spot = (z ^ offset) * helps + (here ^ h_offset)
                resid[i, pl.ds(pl.multiple_of(spot * span, span), span), :] = piece[e, i]
        value = resid[i]
        turned = turn(value.astype(F32), 1.0, -1.0).astype(BF16)
        left = jnp.concatenate([basis[0, i], basis[1, i]], 1)
        out = jnp.dot(left, jnp.concatenate([value, turned], 0), preferred_element_type=F32)
        for j in range(columns):
            left = ranks[i, j] - here * terms
            part = out[j * terms : (j + 1) * terms]
            back[j, i * terms : (i + 1) * terms, :] = jnp.where(row_index < left, part, 0.0)
    back_out[...] = back[...].astype(BF16)
    adjoint_terms(offsets, back, second, keeps, sends)


def own_kernel(back, second, keep, send):
    adjoint_terms([0], back, second, [keep], [send])


def body(wavefield, basis_factor, second_factor, tile_ranks, observed, amplitude):
    _, columns, quarter, rhs = wavefield.shape
    _, rows, _, terms, tile = basis_factor.shape
    span = observed.shape[2]
    zs, rs, helps = lax.axis_size("col"), lax.axis_size("row"), lax.axis_size("help")
    width = 2 * rhs // CHUNKS
    bits = zs.bit_length() - 1
    far = zs // 2
    near = [1 << b for b in range(bits - 1)]
    z_offsets = [int(format(n, f"0{bits}b")[::-1], 2) for n in range(zs)]

    def share(pieces):
        return pieces + [swap("help", d, m) for d in range(1, helps) for m in pieces]

    first = 5 * columns // 8
    shapes = [((n, quarter, width), BF16) for n in (first, columns - first, columns)]
    head, data = call(
        first_kernel,
        "first_waves",
        shapes[:1] + [((3, rows, span, rhs), BF16)],
        [in_hbm(wavefield), in_hbm(observed), in_hbm(amplitude)],
        in_specs=[HBM] * 3,
        scratch=[pltpu.VMEM((2, first, quarter, rhs), BF16), pltpu.SemaphoreType.DMA((4,))],
    )
    data = call(relay_kernel, "relay_data", [(data.shape, BF16)], [after(data, head)], cost=LARGE)[0]
    data = [data, swap("col", far, data)]
    rest, whole, *others = call(
        waves_kernel,
        "other_waves",
        shapes[1:] + shapes[2:] * (CHUNKS - 1),
        [after(wavefield, data[0])],
        cost=LARGE,
    )
    waves = [[head, rest]] + [[w] for w in others]
    gathered = [[[swap("row", d, w) for w in ws] for d in range(1, rs)] for ws in waves]
    wholes = [whole, *others]

    second, basis = call(
        load_kernel,
        "load_factors",
        [((columns, 2 * rows, terms, tile), BF16), ((2, rows, columns, terms, tile), BF16)],
        [second_factor, basis_factor],
        in_specs=[HBM] * 2,
        scratch=[pltpu.SemaphoreType.DMA((2, 2 * rows))],
        cost=LARGE,
    )
    second = second.reshape(columns, 2 * rows * terms, tile)
    basis = basis.reshape(2, rows, columns * terms, tile)
    nears = call(
        near_kernel,
        "near_products",
        [((rows, columns * terms, width), F32)] * CHUNKS,
        [second, *[m for w in wholes for m in share([w])]],
        scratch=[pltpu.VMEM((columns, tile, width), BF16)],
        limit=16 * MIB,
        cost=1,
    )

    def forward(c, mine, heads):
        split = zs if c else SPLIT
        shape, piece = (zs, rows, span, width), (zs // split, rows, span, width)
        pieces = [m for slot in mine for m in slot]
        n = sum(m.shape[0] for m in mine[0])
        return call(
            functools.partial(forward_kernel, z_offsets, [len(slot) for slot in mine], len(heads)),
            "forward_product",
            [(shape, F32)] + [(piece, BF16)] * split,
            [tile_ranks, *pieces, second, basis, nears[c], *heads],
            in_specs=[SM] + [VM] * (len(pieces) + 3 + len(heads)),
            scratch=[
                pltpu.VMEM((n, tile, width), BF16),
                pltpu.VMEM((rows, n * terms, width), F32),
                pltpu.VMEM((rows, tile, width), F32),
            ],
            limit=16 * MIB,
            cost=LARGE if c else 1,
        )

    def backward(c, pieces, spots):
        whole, parts = (columns, width, quarter), 2
        piece = (columns // parts, width, quarter)
        back, *outs = call(
            functools.partial(adjoint_kernel, list(range(1, rs)), spots),
            "adjoint_product",
            [((columns, rows * terms, width), BF16)]
            + [(whole, F32)] * (rs - 1)
            + [(piece, BF16)] * ((rs - 1) * parts),
            [tile_ranks, *pieces, basis, second],
            in_specs=[SM] + [VM] * (len(pieces) + 2),
            scratch=[
                pltpu.VMEM((rows, tile, width), BF16),
                pltpu.VMEM((columns, rows * terms, width), F32),
            ],
            limit=16 * MIB,
            cost=1,
        )
        keeps, sends = outs[: rs - 1], outs[rs - 1 :]
        own = call(
            own_kernel, "own_quarter", [(whole, F32), (whole, BF16)], [back, second], limit=16 * MIB, cost=OWN
        )
        return [own[0], *keeps], [own[1:]] + [sends[d * parts : (d + 1) * parts] for d in range(rs - 1)]

    mirrored, residuals, sent, totals, joined = [], [], [], [], []

    def front(c):
        earlier = [(mirrored[-1][1],)] if c else [(second, *nears), (second, data[1])]
        far_pieces = [[after(m, *e) for m, e in zip(slot, earlier)] for slot in gathered[c]]
        mine = list(far_pieces)
        for d in range(1, helps):
            mine.extend([swap("help", d, m) for m in slot] for slot in far_pieces)
        heads = []
        if c:
            mine[0][0] = after(mine[0][0], mirrored[-1][1])
        else:
            pieces = [slot[0] for slot in mine]
            heads = call(
                functools.partial(head_kernel, [1] * len(pieces)),
                "first_coefficients",
                [((rows, first * terms, width), F32)],
                [tile_ranks, *pieces, second, nears[0]],
                in_specs=[SM] + [VM] * (len(pieces) + 2),
                scratch=[pltpu.VMEM((first, tile, width), BF16)],
                limit=16 * MIB,
                cost=HEAD,
            )
            mine = [slot[1:] or slot for slot in mine]
        keep, *sends = forward(c, mine, heads)
        others = [swap("help", 1, send) for send in sends]
        kernel, stay = mirror_kernel, []
        if len(near) == 1:
            kernel, n = stay_kernel, len(others) // 2
            shape = (keep.shape[0] // 2, rows, span, width)
            stay, others = others[:n], others[n:]
            send = call(sums_kernel, "halve", [(shape, BF16)], [keep, *others], cost=1)[0]
            others = [swap("col", near[0], send)]
        else:
            for d in near:
                shape = (keep.shape[0] // 2, rows, span, width)
                keep, send = call(halve_kernel, "halve", [(shape, F32), (shape, BF16)], [keep, *others], cost=1)
                others = [swap("col", d, send)]
        if c:
            residual_of(c - 1, send)
            keep = after(keep, *residuals[c - 1])
        shape = (2, rows, span, width)
        mirrored.append(
            call(kernel, "mirror", [(shape, F32), (shape, BF16)], [keep, *stay, *others])
        )

    def residual_of(c, *earlier):
        keep, send = mirrored[c]
        residuals.append(
            call(
                functools.partial(residual_kernel, c),
                "residual",
                [((2, rows, span, width), BF16)],
                [after(keep, *earlier), swap("col", far, send), *data],
                cost=LARGE,
            )
        )

    def rear(c):
        pieces, offsets = list(residuals[c]), [[0, far]]
        for d in reversed(near):
            pieces = pieces + [swap("col", d, m) for m in pieces]
            offsets = offsets + [[o ^ d for o in os] for os in offsets]
        last = c + 1 == CHUNKS
        earlier = sent if last else [mirrored[c + 1][1]]
        pieces[1:] = [after(m, *earlier) for m in pieces[1:]]
        passed = list(pieces)
        if not last:
            block = ((1, rows, span, width), BF16)
            for m in pieces[1:]:
                passed.extend(call(spread_kernel, "spread", [block] * 2, [m], cost=1))
            passed[1 : len(pieces)] = []
            passed_offsets = offsets[:1] + [[o] for os in offsets[1:] for o in os]
        else:
            passed_offsets = offsets
        pieces = pieces + [swap("help", d, m) for d in range(1, helps) for m in passed]
        spots = [(o, 0) for o in offsets] + [(o, e) for e in range(1, helps) for o in passed_offsets]
        if not last:
            pieces[0] = after(pieces[0], mirrored[c + 1][1])
        else:
            joined.extend(call(join_kernel, "join", [(observed.shape, BF16)], [r[0] for r in residuals]))
            pieces[0] = after(pieces[0], *joined)
        keeps, sends = backward(c, pieces, spots)
        if not last:
            residual_of(c + 1, sends[0][0])
            keeps = [keeps[0]] + [after(k, *residuals[c + 1]) for k in keeps[1:]]
        shape = (columns, width, quarter)
        shared = [
            call(
                share_kernel,
                "adjoint_share",
                [(shape, BF16)],
                [k, *[swap("help", 1, m) for m in s]],
            )[0]
            for k, s in zip(keeps[1:], sends[1:])
        ]
        if last:
            totals[-1][0] = after(totals[-1][0], *shared)
            mine, theirs, *others = totals[-1]
            mine = call(total_kernel, "total", [(shape, F32)], [mine, *others], cost=1)[0]
            totals[-1] = call(total_kernel, "total", [(shape, F32)], [mine, theirs], cost=LARGE)
        else:
            sent.extend(shared)
        totals.append(
            [keeps[0], swap("help", 1, after(sends[0][0], *shared))]
            + [swap("row", d + 1, m) for d, m in enumerate(shared)]
        )

    for c in range(CHUNKS):
        front(c)
    for c in range(CHUNKS):
        rear(c)

    adjoint = call(
        final_kernel,
        "adjoint_sum",
        [(wavefield.shape, BF16)],
        [*totals[0], *totals[1]],
        out_specs=[HBM],
        scratch=[pltpu.VMEM(wavefield.shape, BF16), pltpu.SemaphoreType.DMA((4,))],
    )[0]
    return joined[0], adjoint


def solution(mesh):
    return jax.shard_map(
        body,
        mesh=mesh,
        in_specs=(
            P("freq", "col", ("row", "help"), None),
            P("freq", "row", "col", "help", None),
            P("freq", "row", "col", "help", None),
            P(("freq", "row"), "col"),
            P("freq", "row", ("col", "help"), None),
            P(("freq", "row"), ("col", "help"), None),
        ),
        out_specs=(
            P("freq", "row", ("col", "help"), None),
            P("freq", "col", ("row", "help"), None),
        ),
        check_vma=False,
    )
```

```python
import functools

import jax
import jax.numpy as jnp
from jax import lax
from jax.experimental import pallas as pl
from jax.experimental.pallas import tpu as pltpu
from jax.sharding import PartitionSpec as P

BF16 = jnp.bfloat16
F32 = jnp.float32
CHUNKS = 2
LANES = 128
VM = pl.BlockSpec(memory_space=pltpu.VMEM)
SM = pl.BlockSpec(memory_space=pltpu.SMEM)
HBM = pl.BlockSpec(memory_space=pltpu.HBM)
ANY = pl.BlockSpec(memory_space=pl.ANY)
MIB = 1024 * 1024
LARGE = 10**10
SPLIT = 2
HEAD = 1
OWN = 1


def call(kernel, name, outs, ins, in_specs=None, out_specs=None, scratch=(), limit=6 * MIB, cost=10**6):
    return pl.pallas_call(
        kernel,
        out_shape=[jax.ShapeDtypeStruct(shape, kind) for shape, kind in outs],
        in_specs=in_specs or [VM] * len(ins),
        out_specs=out_specs or [VM] * len(outs),
        scratch_shapes=list(scratch),
        compiler_params=pltpu.CompilerParams(vmem_limit_bytes=limit),
        cost_estimate=pl.CostEstimate(flops=cost, bytes_accessed=10**4, transcendentals=0),
        name=name,
    )(*ins)


def in_hbm(value):
    return pltpu.with_memory_space_constraint(value, pltpu.HBM)


def swap(axis_name, step, value):
    size = lax.axis_size(axis_name)
    return lax.ppermute(value, axis_name, [(i, i ^ step) for i in range(size)])


def after(value, *earlier):
    return lax.optimization_barrier((value, *earlier))[0]


def turn(value, first, second):
    width = value.shape[-1]
    lane = lax.broadcasted_iota(jnp.int32, value.shape, value.ndim - 1)
    sign = jnp.where(lane < width // 2, first, second).astype(F32)
    return pltpu.roll(value, width // 2, value.ndim - 1) * sign


def side_by_side(source, j, c, part):
    lanes = slice(c * part, (c + 1) * part)
    return jnp.concatenate([source[0, j, :, lanes], source[1, j, :, lanes]], -1)


def first_kernel(source, observed, amplitude, out, data, held, sems):
    n = out.shape[0]
    copies = [pltpu.make_async_copy(source.at[p, :n], held.at[p], sems.at[p]) for p in range(2)]
    copies.append(pltpu.make_async_copy(observed, data.at[:2], sems.at[2]))
    copies.append(pltpu.make_async_copy(amplitude, data.at[2], sems.at[3]))
    for copy in copies:
        copy.start()
    for copy in copies[:2]:
        copy.wait()
    for j in range(n):
        out[j] = side_by_side(held, j, 0, out.shape[-1] // 2)
    for copy in copies[2:]:
        copy.wait()


def relay_kernel(source, out):
    out[...] = source[...]


def waves_kernel(source, rest, whole, *others):
    columns, part = whole.shape[0], whole.shape[-1] // 2
    first = columns - rest.shape[0]
    for j in range(columns):
        whole[j] = side_by_side(source, j, 0, part)
        if j >= first:
            rest[j - first] = whole[j]
        for c, other in enumerate(others):
            other[j] = side_by_side(source, j, c + 1, part)


def load_kernel(second_in, basis_in, second, basis, sems):
    rows = second_in.shape[1]
    copies = []
    for p in range(2):
        for i in range(rows):
            n = p * rows + i
            copies.append(pltpu.make_async_copy(second_in.at[p, i], second.at[:, n], sems.at[0, n]))
            copies.append(pltpu.make_async_copy(basis_in.at[p, i], basis.at[p, i], sems.at[1, n]))
    for copy in copies:
        copy.start()
    for copy in copies:
        copy.wait()


def halve_kernel(mine, *refs):
    others, keep, send = refs[:-2], refs[-2], refs[-1]
    n = keep.shape[0]
    total = jnp.concatenate([other[...] for other in others], 0).astype(F32) + mine[...]
    keep[...] = total[:n]
    send[...] = total[n:].astype(BF16)


def sums_kernel(mine, *refs):
    others, send = refs[:-1], refs[-1]
    n = send.shape[0]
    total = jnp.concatenate([other[...] for other in others], 0).astype(F32) + mine[n:]
    send[...] = total.astype(BF16)


def stay_kernel(mine, *refs):
    *others, arrived, keep, send = refs
    n = keep.shape[0]
    total = jnp.concatenate([other[...] for other in others], 0).astype(F32) + mine[:n]
    total = total + arrived[...].astype(F32)
    keep[...] = total
    for e in range(n):
        send[e] = total[n - 1 - e].astype(BF16)


def mirror_kernel(mine, *refs):
    others, keep, send = refs[:-2], refs[-2], refs[-1]
    total = jnp.concatenate([other[...] for other in others], 0).astype(F32) + mine[...]
    keep[...] = total
    n = keep.shape[0]
    for e in range(n):
        send[e] = total[n - 1 - e].astype(BF16)


def residual_kernel(c, mine, other, *refs):
    arrays, out = refs[:2], refs[2]
    part = out.shape[-1] // 2
    lanes = slice(c * part, (c + 1) * part)
    for e in range(2):
        total = mine[e] + other[e].astype(F32)
        data = jnp.concatenate([arrays[e][p, :, :, lanes] for p in range(2)], -1)
        weight = jnp.concatenate([arrays[e][2, :, :, lanes]] * 2, -1)
        value = (weight.astype(F32) * (total - data.astype(F32))).astype(BF16)
        out[e] = value


def spread_kernel(source, *outs):
    for e, out in enumerate(outs):
        out[0] = source[e]


def join_kernel(*refs):
    out = refs[-1]
    part = out.shape[-1] // (len(refs) - 1)
    for p in range(2):
        out[p] = jnp.concatenate([ref[0, :, :, p * part : (p + 1) * part] for ref in refs[:-1]], -1)


def share_kernel(mine, *refs):
    others, out = refs[:-1], refs[-1]
    n = others[0].shape[0]
    for k, other in enumerate(others):
        at = slice(k * n, (k + 1) * n)
        out[at] = (mine[at] + other[...].astype(F32)).astype(BF16)


def total_kernel(mine, *refs):
    others, out = refs[:-1], refs[-1]
    total = mine[...]
    for ref in others:
        total = total + ref[...].astype(F32)
    out[...] = total


def final_kernel(done, mine, *refs):
    *others, out, out_ref, sems = refs
    part = mine.shape[1] // 2
    columns = out_ref.shape[1]
    copies = []
    for j in range(columns):
        for p in range(2):
            lanes = slice(p * part, (p + 1) * part)
            total = mine[j, lanes, :]
            for ref in others:
                total = total + ref[j, lanes, :].astype(F32)
            out_ref[p, j] = jnp.concatenate([done[j, lanes, :], total], 0).astype(out_ref.dtype).T
        n = len(copies)
        if j + 1 == (n + 1) * columns // sems.shape[0]:
            at = slice(n * columns // sems.shape[0], j + 1)
            copies.append(pltpu.make_async_copy(out_ref.at[:, at], out.at[:, at], sems.at[n]))
            copies[-1].start()
    for copy in copies:
        copy.wait()


def slots_of(counts, refs):
    slots, at = [], 0
    for count in counts:
        slots.append([(ref, j) for ref in refs[at : at + count] for j in range(ref.shape[0])])
        at += count
    return slots, refs[at:]


def products(slots, places, columns, second, waves):
    _, quarter, width = slots[0][0][0].shape
    half = second.shape[1] // 2
    at_all = [pl.multiple_of(at * quarter, quarter) for at in places]
    for n, j in enumerate(columns):
        parts = [ref[k] for ref, k in (slot[n if len(slot) == len(columns) else j] for slot in slots)]
        if quarter % LANES == 0:
            left = jnp.concatenate([second[j, :, pl.ds(at, quarter)] for at in at_all], 1)
            right = jnp.concatenate(parts, 0)
        else:
            waves[n] = jnp.zeros(waves.shape[1:], BF16)
            for at, part in zip(at_all, parts):
                waves[n, pl.ds(at, quarter), :] = part
            left, right = second[j], waves[n]
        out = jnp.dot(left, right, preferred_element_type=F32)
        yield n, j, out[:half] + turn(out[half:], 1.0, -1.0)


def near_kernel(second, *refs):
    r, here = lax.axis_index("row"), lax.axis_index("help")
    helps = lax.axis_size("help")
    *refs, waves = refs
    parts = len(refs) // (helps + 1)
    for c in range(parts):
        out = refs[parts * helps + c]
        slots = [[(ref, j) for j in range(ref.shape[0])] for ref in refs[c * helps : (c + 1) * helps]]
        places = [r * helps + (here ^ d) for d in range(helps)]
        rows = out.shape[0]
        for n, j, value in products(slots, places, range(second.shape[0]), second, waves):
            terms = value.shape[0] // rows
            for i in range(rows):
                out[i, j * terms : (j + 1) * terms, :] = value[i * terms : (i + 1) * terms]


def coefficients(slots, columns, ranks, second, near, waves, coef):
    rs, helps = lax.axis_size("row"), lax.axis_size("help")
    r, here = lax.axis_index("row"), lax.axis_index("help")
    rows = coef.shape[0]
    terms = second.shape[1] // (2 * rows)
    row_index = lax.broadcasted_iota(jnp.int32, (terms, coef.shape[2]), 0)
    places = [(r ^ d) * helps + (here ^ e) for e in range(helps) for d in range(1, rs)]
    for n, j, value in products(slots, places, columns, second, waves):
        for i in range(rows):
            left = ranks[i, j] - here * terms
            part = value[i * terms : (i + 1) * terms] + near[i, j * terms : (j + 1) * terms, :]
            coef[i, n * terms : (n + 1) * terms, :] = jnp.where(row_index < left, part, 0.0)


def head_kernel(counts, ranks, *refs):
    slots, (second, near, coef, waves) = slots_of(counts, refs)
    coefficients(slots, range(len(slots[0])), ranks, second, near, waves, coef)


def forward_kernel(z_offsets, counts, n_heads, ranks, *refs):
    slots, refs = slots_of(counts, refs)
    (second, basis, near), heads, refs = refs[:3], refs[3 : 3 + n_heads], refs[3 + n_heads :]
    keep_out, *sends, waves, coef, fwd = refs
    n_send = sends[0].shape[0]
    helps = lax.axis_size("help")
    z, here = lax.axis_index("col"), lax.axis_index("help")
    columns = second.shape[0]
    coefficients(slots, range(columns - len(slots[0]), columns), ranks, second, near, waves, coef)
    rows = basis.shape[1]
    _, _, span, _ = keep_out.shape
    dims = (((0,), (0,)), ((), ()))
    for i in range(rows):
        value = jnp.concatenate([head[i] for head in heads] + [coef[i]], 0)
        left = jnp.concatenate([value, turn(value, -1.0, 1.0)], 0).astype(BF16)
        right = jnp.concatenate([basis[0, i], basis[1, i]], 0)
        out = lax.dot_general(left, right, dims, preferred_element_type=F32)
        fwd[i] = out.T
        for n, offset in enumerate(z_offsets):
            block = (z ^ offset) * helps
            at = pl.multiple_of((block + here) * span, span)
            keep_out[n, i] = fwd[i, pl.ds(at, span), :].astype(keep_out.dtype)
            at = pl.multiple_of((block + 1 - here) * span, span)
            sends[n // n_send][n % n_send, i] = fwd[i, pl.ds(at, span), :].astype(BF16)


def adjoint_terms(offsets, back, second, keeps, sends):
    rs, helps = lax.axis_size("row"), lax.axis_size("help")
    r, here = lax.axis_index("row"), lax.axis_index("help")
    _, width, quarter = keeps[0].shape
    parts = len(sends) // len(offsets)
    half = back.shape[1]

    def keep(d, j, value):
        keeps[d][j] = value

    def send(d, j, value):
        refs = sends[d * parts : (d + 1) * parts]
        n = refs[0].shape[0]
        refs[j // n][j % n] = value.astype(BF16)

    for j in range(back.shape[0]):
        real = back[j].astype(BF16).T
        turned = jnp.concatenate([-real[width // 2 :], real[: width // 2]], 0)

        def product(right):
            out = jnp.dot(real, right[:half], preferred_element_type=F32)
            return out + jnp.dot(turned, right[half:], preferred_element_type=F32)

        if quarter % LANES == 0:
            for n, d in enumerate(offsets):
                places = [((r ^ d) * helps + h) * quarter for h in (here, 1 - here)]
                places = [pl.multiple_of(at, quarter) for at in places]
                out = product(jnp.concatenate([second[j, :, pl.ds(at, quarter)] for at in places], 1))
                keep(n, j, out[:, :quarter])
                send(n, j, out[:, quarter:])
        else:
            out = product(second[j])
            for m in range(rs):
                for h in range(helps):
                    part = out[:, (m * helps + h) * quarter : (m * helps + h + 1) * quarter]
                    for n, d in enumerate(offsets):
                        pl.when((here == h) & (m ^ r == d))(functools.partial(keep, n, j, part))
                        pl.when((here != h) & (m ^ r == d))(functools.partial(send, n, j, part))


def adjoint_kernel(offsets, spots, ranks, *refs):
    n_pieces, n = len(spots), len(offsets)
    pieces, (basis, second), refs = refs[:n_pieces], refs[n_pieces : n_pieces + 2], refs[n_pieces + 2 :]
    back_out, keeps, sends, (resid, back) = refs[0], refs[1 : 1 + n], refs[1 + n : -2], refs[-2:]
    helps = lax.axis_size("help")
    z, here = lax.axis_index("col"), lax.axis_index("help")
    _, rows, span, width = pieces[0].shape
    columns = second.shape[0]
    terms = second.shape[1] // (2 * rows)
    row_index = lax.broadcasted_iota(jnp.int32, (terms, width), 0)
    for i in range(rows):
        for piece, (z_offsets, h_offset) in zip(pieces, spots):
            for e, offset in enumerate(z_offsets):
                spot = (z ^ offset) * helps + (here ^ h_offset)
                resid[i, pl.ds(pl.multiple_of(spot * span, span), span), :] = piece[e, i]
        value = resid[i]
        turned = turn(value.astype(F32), 1.0, -1.0).astype(BF16)
        left = jnp.concatenate([basis[0, i], basis[1, i]], 1)
        out = jnp.dot(left, jnp.concatenate([value, turned], 0), preferred_element_type=F32)
        for j in range(columns):
            left = ranks[i, j] - here * terms
            part = out[j * terms : (j + 1) * terms]
            back[j, i * terms : (i + 1) * terms, :] = jnp.where(row_index < left, part, 0.0)
    back_out[...] = back[...].astype(BF16)
    adjoint_terms(offsets, back, second, keeps, sends)


def own_kernel(back, second, keep, send):
    adjoint_terms([0], back, second, [keep], [send])


def body(wavefield, basis_factor, second_factor, tile_ranks, observed, amplitude):
    _, columns, quarter, rhs = wavefield.shape
    _, rows, _, terms, tile = basis_factor.shape
    span = observed.shape[2]
    zs, rs, helps = lax.axis_size("col"), lax.axis_size("row"), lax.axis_size("help")
    width = 2 * rhs // CHUNKS
    bits = zs.bit_length() - 1
    far = zs // 2
    near = [1 << b for b in range(bits - 1)]
    z_offsets = [int(format(n, f"0{bits}b")[::-1], 2) for n in range(zs)]

    def share(pieces):
        return pieces + [swap("help", d, m) for d in range(1, helps) for m in pieces]

    first = 5 * columns // 8
    shapes = [((n, quarter, width), BF16) for n in (first, columns - first, columns)]
    head, data = call(
        first_kernel,
        "first_waves",
        shapes[:1] + [((3, rows, span, rhs), BF16)],
        [in_hbm(wavefield), in_hbm(observed), in_hbm(amplitude)],
        in_specs=[HBM] * 3,
        scratch=[pltpu.VMEM((2, first, quarter, rhs), BF16), pltpu.SemaphoreType.DMA((4,))],
    )
    data = call(relay_kernel, "relay_data", [(data.shape, BF16)], [after(data, head)], cost=LARGE)[0]
    data = [data, swap("col", far, data)]
    rest, whole, *others = call(
        waves_kernel,
        "other_waves",
        shapes[1:] + shapes[2:] * (CHUNKS - 1),
        [after(wavefield, data[0])],
        cost=LARGE,
    )
    waves = [[head, rest]] + [[w] for w in others]
    gathered = [[[swap("row", d, w) for w in ws] for d in range(1, rs)] for ws in waves]
    wholes = [whole, *others]

    second, basis = call(
        load_kernel,
        "load_factors",
        [((columns, 2 * rows, terms, tile), BF16), ((2, rows, columns, terms, tile), BF16)],
        [second_factor, basis_factor],
        in_specs=[HBM] * 2,
        scratch=[pltpu.SemaphoreType.DMA((2, 2 * rows))],
        cost=LARGE,
    )
    second = second.reshape(columns, 2 * rows * terms, tile)
    basis = basis.reshape(2, rows, columns * terms, tile)
    nears = call(
        near_kernel,
        "near_products",
        [((rows, columns * terms, width), F32)] * CHUNKS,
        [second, *[m for w in wholes for m in share([w])]],
        scratch=[pltpu.VMEM((columns, tile, width), BF16)],
        limit=16 * MIB,
        cost=1,
    )

    def forward(c, mine, heads):
        split = zs if c else SPLIT
        shape, piece = (zs, rows, span, width), (zs // split, rows, span, width)
        pieces = [m for slot in mine for m in slot]
        n = sum(m.shape[0] for m in mine[0])
        return call(
            functools.partial(forward_kernel, z_offsets, [len(slot) for slot in mine], len(heads)),
            "forward_product",
            [(shape, F32)] + [(piece, BF16)] * split,
            [tile_ranks, *pieces, second, basis, nears[c], *heads],
            in_specs=[SM] + [VM] * (len(pieces) + 3 + len(heads)),
            scratch=[
                pltpu.VMEM((n, tile, width), BF16),
                pltpu.VMEM((rows, n * terms, width), F32),
                pltpu.VMEM((rows, tile, width), F32),
            ],
            limit=16 * MIB,
            cost=LARGE if c else 1,
        )

    def backward(c, pieces, spots):
        whole, parts = (columns, width, quarter), 2
        piece = (columns // parts, width, quarter)
        back, *outs = call(
            functools.partial(adjoint_kernel, list(range(1, rs)), spots),
            "adjoint_product",
            [((columns, rows * terms, width), BF16)]
            + [(whole, F32)] * (rs - 1)
            + [(piece, BF16)] * ((rs - 1) * parts),
            [tile_ranks, *pieces, basis, second],
            in_specs=[SM] + [VM] * (len(pieces) + 2),
            scratch=[
                pltpu.VMEM((rows, tile, width), BF16),
                pltpu.VMEM((columns, rows * terms, width), F32),
            ],
            limit=16 * MIB,
            cost=1,
        )
        keeps, sends = outs[: rs - 1], outs[rs - 1 :]
        own = call(
            own_kernel, "own_quarter", [(whole, F32), (whole, BF16)], [back, second], limit=16 * MIB, cost=OWN
        )
        return [own[0], *keeps], [own[1:]] + [sends[d * parts : (d + 1) * parts] for d in range(rs - 1)]

    mirrored, residuals, sent, totals, joined = [], [], [], [], []

    def front(c):
        earlier = [(mirrored[-1][1],)] if c else [(second, *nears), (second, data[1])]
        far_pieces = [[after(m, *e) for m, e in zip(slot, earlier)] for slot in gathered[c]]
        mine = list(far_pieces)
        for d in range(1, helps):
            mine.extend([swap("help", d, m) for m in slot] for slot in far_pieces)
        heads = []
        if c:
            mine[0][0] = after(mine[0][0], mirrored[-1][1])
        else:
            pieces = [slot[0] for slot in mine]
            heads = call(
                functools.partial(head_kernel, [1] * len(pieces)),
                "first_coefficients",
                [((rows, first * terms, width), F32)],
                [tile_ranks, *pieces, second, nears[0]],
                in_specs=[SM] + [VM] * (len(pieces) + 2),
                scratch=[pltpu.VMEM((first, tile, width), BF16)],
                limit=16 * MIB,
                cost=HEAD,
            )
            mine = [slot[1:] or slot for slot in mine]
        keep, *sends = forward(c, mine, heads)
        others = [swap("help", 1, send) for send in sends]
        kernel, stay = mirror_kernel, []
        if len(near) == 1:
            kernel, n = stay_kernel, len(others) // 2
            shape = (keep.shape[0] // 2, rows, span, width)
            stay, others = others[:n], others[n:]
            send = call(sums_kernel, "halve", [(shape, BF16)], [keep, *others], cost=1)[0]
            others = [swap("col", near[0], send)]
        else:
            for d in near:
                shape = (keep.shape[0] // 2, rows, span, width)
                keep, send = call(halve_kernel, "halve", [(shape, F32), (shape, BF16)], [keep, *others], cost=1)
                others = [swap("col", d, send)]
        if c:
            residual_of(c - 1, send, *stay)
            keep = after(keep, *residuals[c - 1])
        shape = (2, rows, span, width)
        mirrored.append(
            call(kernel, "mirror", [(shape, F32), (shape, BF16)], [keep, *stay, *others])
        )

    def residual_of(c, *earlier):
        keep, send = mirrored[c]
        residuals.append(
            call(
                functools.partial(residual_kernel, c),
                "residual",
                [((2, rows, span, width), BF16)],
                [after(keep, *earlier), swap("col", far, send), *data],
                cost=LARGE,
            )
        )

    def rear(c):
        pieces, offsets = list(residuals[c]), [[0, far]]
        for d in reversed(near):
            pieces = pieces + [swap("col", d, m) for m in pieces]
            offsets = offsets + [[o ^ d for o in os] for os in offsets]
        last = c + 1 == CHUNKS
        earlier = sent if last else [mirrored[c + 1][1]]
        pieces[1:] = [after(m, *earlier) for m in pieces[1:]]
        passed = list(pieces)
        if not last:
            block = ((1, rows, span, width), BF16)
            for m in pieces[1:]:
                passed.extend(call(spread_kernel, "spread", [block] * 2, [m], cost=1))
            passed[1 : len(pieces)] = []
            passed_offsets = offsets[:1] + [[o] for os in offsets[1:] for o in os]
        else:
            passed_offsets = offsets
        pieces = pieces + [swap("help", d, m) for d in range(1, helps) for m in passed]
        spots = [(o, 0) for o in offsets] + [(o, e) for e in range(1, helps) for o in passed_offsets]
        if not last:
            pieces[0] = after(pieces[0], mirrored[c + 1][1])
        else:
            joined.extend(call(join_kernel, "join", [(observed.shape, BF16)], [r[0] for r in residuals]))
            pieces[0] = after(pieces[0], *joined)
        keeps, sends = backward(c, pieces, spots)
        if not last:
            residual_of(c + 1, sends[0][0])
            keeps = [keeps[0]] + [after(k, *residuals[c + 1]) for k in keeps[1:]]
        shape = (columns, width, quarter)
        shared = [
            call(
                share_kernel,
                "adjoint_share",
                [(shape, BF16)],
                [k, *[swap("help", 1, m) for m in s]],
            )[0]
            for k, s in zip(keeps[1:], sends[1:])
        ]
        if last:
            totals[-1][0] = after(totals[-1][0], *shared)
            mine, theirs, *others = totals[-1]
            mine = call(total_kernel, "total", [(shape, F32)], [mine, *others], cost=1)[0]
            totals[-1] = call(total_kernel, "total", [(shape, F32)], [mine, theirs], cost=LARGE)
        else:
            sent.extend(shared)
        totals.append(
            [keeps[0], swap("help", 1, after(sends[0][0], *shared))]
            + [swap("row", d + 1, m) for d, m in enumerate(shared)]
        )

    for c in range(CHUNKS):
        front(c)
    for c in range(CHUNKS):
        rear(c)

    adjoint = call(
        final_kernel,
        "adjoint_sum",
        [(wavefield.shape, BF16)],
        [*totals[0], *totals[1]],
        out_specs=[HBM],
        scratch=[pltpu.VMEM(wavefield.shape, BF16), pltpu.SemaphoreType.DMA((4,))],
    )[0]
    return joined[0], adjoint


def solution(mesh):
    return jax.shard_map(
        body,
        mesh=mesh,
        in_specs=(
            P("freq", "col", ("row", "help"), None),
            P("freq", "row", "col", "help", None),
            P("freq", "row", "col", "help", None),
            P(("freq", "row"), "col"),
            P("freq", "row", ("col", "help"), None),
            P(("freq", "row"), ("col", "help"), None),
        ),
        out_specs=(
            P("freq", "row", ("col", "help"), None),
            P("freq", "col", ("row", "help"), None),
        ),
        check_vma=False,
    )
```

```python
import functools

import jax
import jax.numpy as jnp
from jax import lax
from jax.experimental import pallas as pl
from jax.experimental.pallas import tpu as pltpu
from jax.sharding import PartitionSpec as P

BF16 = jnp.bfloat16
F32 = jnp.float32
CHUNKS = 2
LANES = 128
VM = pl.BlockSpec(memory_space=pltpu.VMEM)
SM = pl.BlockSpec(memory_space=pltpu.SMEM)
HBM = pl.BlockSpec(memory_space=pltpu.HBM)
ANY = pl.BlockSpec(memory_space=pl.ANY)
MIB = 1024 * 1024
LARGE = 10**10
SPLIT = 2
HEAD = 1
OWN = 1


def call(kernel, name, outs, ins, in_specs=None, out_specs=None, scratch=(), limit=6 * MIB, cost=10**6):
    return pl.pallas_call(
        kernel,
        out_shape=[jax.ShapeDtypeStruct(shape, kind) for shape, kind in outs],
        in_specs=in_specs or [VM] * len(ins),
        out_specs=out_specs or [VM] * len(outs),
        scratch_shapes=list(scratch),
        compiler_params=pltpu.CompilerParams(vmem_limit_bytes=limit),
        cost_estimate=pl.CostEstimate(flops=cost, bytes_accessed=10**4, transcendentals=0),
        name=name,
    )(*ins)


def in_hbm(value):
    return pltpu.with_memory_space_constraint(value, pltpu.HBM)


def swap(axis_name, step, value):
    size = lax.axis_size(axis_name)
    return lax.ppermute(value, axis_name, [(i, i ^ step) for i in range(size)])


def after(value, *earlier):
    return lax.optimization_barrier((value, *earlier))[0]


def turn(value, first, second):
    width = value.shape[-1]
    lane = lax.broadcasted_iota(jnp.int32, value.shape, value.ndim - 1)
    sign = jnp.where(lane < width // 2, first, second).astype(F32)
    return pltpu.roll(value, width // 2, value.ndim - 1) * sign


def side_by_side(source, j, c, part):
    lanes = slice(c * part, (c + 1) * part)
    return jnp.concatenate([source[0, j, :, lanes], source[1, j, :, lanes]], -1)


def first_kernel(source, observed, amplitude, out, data, held, sems):
    n = out.shape[0]
    copies = [pltpu.make_async_copy(source.at[p, :n], held.at[p], sems.at[p]) for p in range(2)]
    copies.append(pltpu.make_async_copy(observed, data.at[:2], sems.at[2]))
    copies.append(pltpu.make_async_copy(amplitude, data.at[2], sems.at[3]))
    for copy in copies:
        copy.start()
    for copy in copies[:2]:
        copy.wait()
    for j in range(n):
        out[j] = side_by_side(held, j, 0, out.shape[-1] // 2)
    for copy in copies[2:]:
        copy.wait()


def relay_kernel(source, out):
    out[...] = source[...]


def waves_kernel(source, rest, whole, *others):
    columns, part = whole.shape[0], whole.shape[-1] // 2
    first = columns - rest.shape[0]
    for j in range(columns):
        whole[j] = side_by_side(source, j, 0, part)
        if j >= first:
            rest[j - first] = whole[j]
        for c, other in enumerate(others):
            other[j] = side_by_side(source, j, c + 1, part)


def load_kernel(second_in, basis_in, second, basis, sems):
    rows = second_in.shape[1]
    copies = []
    for p in range(2):
        for i in range(rows):
            n = p * rows + i
            copies.append(pltpu.make_async_copy(second_in.at[p, i], second.at[:, n], sems.at[0, n]))
            copies.append(pltpu.make_async_copy(basis_in.at[p, i], basis.at[p, i], sems.at[1, n]))
    for copy in copies:
        copy.start()
    for copy in copies:
        copy.wait()


def halve_kernel(mine, *refs):
    others, keep, send = refs[:-2], refs[-2], refs[-1]
    n = keep.shape[0]
    total = jnp.concatenate([other[...] for other in others], 0).astype(F32) + mine[...]
    keep[...] = total[:n]
    send[...] = total[n:].astype(BF16)


def sums_kernel(mine, *refs):
    others, send = refs[:-1], refs[-1]
    n = send.shape[0]
    total = jnp.concatenate([other[...] for other in others], 0).astype(F32) + mine[n:]
    send[...] = total.astype(BF16)


def stay_kernel(mine, *refs):
    *others, arrived, keep, send = refs
    n = keep.shape[0]
    total = jnp.concatenate([other[...] for other in others], 0).astype(F32) + mine[:n]
    total = total + arrived[...].astype(F32)
    keep[...] = total
    for e in range(n):
        send[e] = total[n - 1 - e].astype(BF16)


def mirror_kernel(mine, *refs):
    others, keep, send = refs[:-2], refs[-2], refs[-1]
    total = jnp.concatenate([other[...] for other in others], 0).astype(F32) + mine[...]
    keep[...] = total
    n = keep.shape[0]
    for e in range(n):
        send[e] = total[n - 1 - e].astype(BF16)


def residual_kernel(c, mine, other, *refs):
    arrays, out = refs[:2], refs[2]
    part = out.shape[-1] // 2
    lanes = slice(c * part, (c + 1) * part)
    for e in range(2):
        total = mine[e] + other[e].astype(F32)
        data = jnp.concatenate([arrays[e][p, :, :, lanes] for p in range(2)], -1)
        weight = jnp.concatenate([arrays[e][2, :, :, lanes]] * 2, -1)
        value = (weight.astype(F32) * (total - data.astype(F32))).astype(BF16)
        out[e] = value


def spread_kernel(source, *outs):
    for e, out in enumerate(outs):
        out[0] = source[e]


def join_kernel(*refs):
    out = refs[-1]
    part = out.shape[-1] // (len(refs) - 1)
    for p in range(2):
        out[p] = jnp.concatenate([ref[0, :, :, p * part : (p + 1) * part] for ref in refs[:-1]], -1)


def share_kernel(mine, *refs):
    others, out = refs[:-1], refs[-1]
    n = others[0].shape[0]
    for k, other in enumerate(others):
        at = slice(k * n, (k + 1) * n)
        out[at] = (mine[at] + other[...].astype(F32)).astype(BF16)


def total_kernel(mine, *refs):
    others, out = refs[:-1], refs[-1]
    total = mine[...]
    for ref in others:
        total = total + ref[...].astype(F32)
    out[...] = total


def final_kernel(done, mine, *refs):
    *others, out, out_ref, sems = refs
    part = mine.shape[1] // 2
    columns = out_ref.shape[1]
    copies = []
    for j in range(columns):
        for p in range(2):
            lanes = slice(p * part, (p + 1) * part)
            total = mine[j, lanes, :]
            for ref in others:
                total = total + ref[j, lanes, :].astype(F32)
            out_ref[p, j] = jnp.concatenate([done[j, lanes, :], total], 0).astype(out_ref.dtype).T
        n = len(copies)
        if j + 1 == (n + 1) * columns // sems.shape[0]:
            at = slice(n * columns // sems.shape[0], j + 1)
            copies.append(pltpu.make_async_copy(out_ref.at[:, at], out.at[:, at], sems.at[n]))
            copies[-1].start()
    for copy in copies:
        copy.wait()


def slots_of(counts, refs):
    slots, at = [], 0
    for count in counts:
        slots.append([(ref, j) for ref in refs[at : at + count] for j in range(ref.shape[0])])
        at += count
    return slots, refs[at:]


def products(slots, places, columns, second, waves):
    _, quarter, width = slots[0][0][0].shape
    half = second.shape[1] // 2
    at_all = [pl.multiple_of(at * quarter, quarter) for at in places]
    for n, j in enumerate(columns):
        parts = [ref[k] for ref, k in (slot[n if len(slot) == len(columns) else j] for slot in slots)]
        if quarter % LANES == 0:
            left = jnp.concatenate([second[j, :, pl.ds(at, quarter)] for at in at_all], 1)
            right = jnp.concatenate(parts, 0)
        else:
            waves[n] = jnp.zeros(waves.shape[1:], BF16)
            for at, part in zip(at_all, parts):
                waves[n, pl.ds(at, quarter), :] = part
            left, right = second[j], waves[n]
        out = jnp.dot(left, right, preferred_element_type=F32)
        yield n, j, out[:half] + turn(out[half:], 1.0, -1.0)


def near_kernel(second, *refs):
    r, here = lax.axis_index("row"), lax.axis_index("help")
    helps = lax.axis_size("help")
    *refs, waves = refs
    parts = len(refs) // (helps + 1)
    for c in range(parts):
        out = refs[parts * helps + c]
        slots = [[(ref, j) for j in range(ref.shape[0])] for ref in refs[c * helps : (c + 1) * helps]]
        places = [r * helps + (here ^ d) for d in range(helps)]
        rows = out.shape[0]
        for n, j, value in products(slots, places, range(second.shape[0]), second, waves):
            terms = value.shape[0] // rows
            for i in range(rows):
                out[i, j * terms : (j + 1) * terms, :] = value[i * terms : (i + 1) * terms]


def coefficients(slots, columns, ranks, second, near, waves, coef):
    rs, helps = lax.axis_size("row"), lax.axis_size("help")
    r, here = lax.axis_index("row"), lax.axis_index("help")
    rows = coef.shape[0]
    terms = second.shape[1] // (2 * rows)
    row_index = lax.broadcasted_iota(jnp.int32, (terms, coef.shape[2]), 0)
    places = [(r ^ d) * helps + (here ^ e) for e in range(helps) for d in range(1, rs)]
    for n, j, value in products(slots, places, columns, second, waves):
        for i in range(rows):
            left = ranks[i, j] - here * terms
            part = value[i * terms : (i + 1) * terms] + near[i, j * terms : (j + 1) * terms, :]
            coef[i, n * terms : (n + 1) * terms, :] = jnp.where(row_index < left, part, 0.0)


def head_kernel(counts, ranks, *refs):
    slots, (second, near, coef, waves) = slots_of(counts, refs)
    coefficients(slots, range(len(slots[0])), ranks, second, near, waves, coef)


def forward_kernel(z_offsets, counts, n_heads, ranks, *refs):
    slots, refs = slots_of(counts, refs)
    (second, basis, near), heads, refs = refs[:3], refs[3 : 3 + n_heads], refs[3 + n_heads :]
    keep_out, *sends, waves, coef, fwd = refs
    n_send = sends[0].shape[0]
    helps = lax.axis_size("help")
    z, here = lax.axis_index("col"), lax.axis_index("help")
    columns = second.shape[0]
    coefficients(slots, range(columns - len(slots[0]), columns), ranks, second, near, waves, coef)
    rows = basis.shape[1]
    _, _, span, _ = keep_out.shape
    dims = (((0,), (0,)), ((), ()))
    for i in range(rows):
        value = jnp.concatenate([head[i] for head in heads] + [coef[i]], 0)
        left = jnp.concatenate([value, turn(value, -1.0, 1.0)], 0).astype(BF16)
        right = jnp.concatenate([basis[0, i], basis[1, i]], 0)
        out = lax.dot_general(left, right, dims, preferred_element_type=F32)
        fwd[i] = out.T
        for n, offset in enumerate(z_offsets):
            block = (z ^ offset) * helps
            at = pl.multiple_of((block + here) * span, span)
            keep_out[n, i] = fwd[i, pl.ds(at, span), :].astype(keep_out.dtype)
            at = pl.multiple_of((block + 1 - here) * span, span)
            sends[n // n_send][n % n_send, i] = fwd[i, pl.ds(at, span), :].astype(BF16)


def adjoint_terms(offsets, back, second, keeps, sends, rounded=None):
    rs, helps = lax.axis_size("row"), lax.axis_size("help")
    r, here = lax.axis_index("row"), lax.axis_index("help")
    _, width, quarter = keeps[0].shape
    parts = len(sends) // len(offsets)
    half = back.shape[1]

    def keep(d, j, value):
        keeps[d][j] = value

    def send(d, j, value):
        refs = sends[d * parts : (d + 1) * parts]
        n = refs[0].shape[0]
        refs[j // n][j % n] = value.astype(BF16)

    for j in range(back.shape[0]):
        value = back[j].astype(BF16)
        if rounded is not None:
            rounded[j] = value
        real = value.T
        turned = jnp.concatenate([-real[width // 2 :], real[: width // 2]], 0)

        def product(right):
            out = jnp.dot(real, right[:half], preferred_element_type=F32)
            return out + jnp.dot(turned, right[half:], preferred_element_type=F32)

        if quarter % LANES == 0:
            for n, d in enumerate(offsets):
                places = [((r ^ d) * helps + h) * quarter for h in (here, 1 - here)]
                places = [pl.multiple_of(at, quarter) for at in places]
                out = product(jnp.concatenate([second[j, :, pl.ds(at, quarter)] for at in places], 1))
                keep(n, j, out[:, :quarter])
                send(n, j, out[:, quarter:])
        else:
            out = product(second[j])
            for m in range(rs):
                for h in range(helps):
                    part = out[:, (m * helps + h) * quarter : (m * helps + h + 1) * quarter]
                    for n, d in enumerate(offsets):
                        pl.when((here == h) & (m ^ r == d))(functools.partial(keep, n, j, part))
                        pl.when((here != h) & (m ^ r == d))(functools.partial(send, n, j, part))


def adjoint_kernel(offsets, spots, ranks, *refs):
    n_pieces, n = len(spots), len(offsets)
    pieces, (basis, second), refs = refs[:n_pieces], refs[n_pieces : n_pieces + 2], refs[n_pieces + 2 :]
    back_out, keeps, sends, (resid, back) = refs[0], refs[1 : 1 + n], refs[1 + n : -2], refs[-2:]
    helps = lax.axis_size("help")
    z, here = lax.axis_index("col"), lax.axis_index("help")
    _, rows, span, width = pieces[0].shape
    columns = second.shape[0]
    terms = second.shape[1] // (2 * rows)
    row_index = lax.broadcasted_iota(jnp.int32, (terms, width), 0)
    for i in range(rows):
        for piece, (z_offsets, h_offset) in zip(pieces, spots):
            for e, offset in enumerate(z_offsets):
                spot = (z ^ offset) * helps + (here ^ h_offset)
                resid[i, pl.ds(pl.multiple_of(spot * span, span), span), :] = piece[e, i]
        value = resid[i]
        turned = turn(value.astype(F32), 1.0, -1.0).astype(BF16)
        left = jnp.concatenate([basis[0, i], basis[1, i]], 1)
        out = jnp.dot(left, jnp.concatenate([value, turned], 0), preferred_element_type=F32)
        for j in range(columns):
            left = ranks[i, j] - here * terms
            part = out[j * terms : (j + 1) * terms]
            back[j, i * terms : (i + 1) * terms, :] = jnp.where(row_index < left, part, 0.0)
    adjoint_terms(offsets, back, second, keeps, sends, back_out)


def own_kernel(back, second, keep, send):
    adjoint_terms([0], back, second, [keep], [send])


def body(wavefield, basis_factor, second_factor, tile_ranks, observed, amplitude):
    _, columns, quarter, rhs = wavefield.shape
    _, rows, _, terms, tile = basis_factor.shape
    span = observed.shape[2]
    zs, rs, helps = lax.axis_size("col"), lax.axis_size("row"), lax.axis_size("help")
    width = 2 * rhs // CHUNKS
    bits = zs.bit_length() - 1
    far = zs // 2
    near = [1 << b for b in range(bits - 1)]
    z_offsets = [int(format(n, f"0{bits}b")[::-1], 2) for n in range(zs)]

    def share(pieces):
        return pieces + [swap("help", d, m) for d in range(1, helps) for m in pieces]

    first = 5 * columns // 8
    shapes = [((n, quarter, width), BF16) for n in (first, columns - first, columns)]
    head, data = call(
        first_kernel,
        "first_waves",
        shapes[:1] + [((3, rows, span, rhs), BF16)],
        [in_hbm(wavefield), in_hbm(observed), in_hbm(amplitude)],
        in_specs=[HBM] * 3,
        scratch=[pltpu.VMEM((2, first, quarter, rhs), BF16), pltpu.SemaphoreType.DMA((4,))],
    )
    data = call(relay_kernel, "relay_data", [(data.shape, BF16)], [after(data, head)], cost=LARGE)[0]
    data = [data, swap("col", far, data)]
    rest, whole, *others = call(
        waves_kernel,
        "other_waves",
        shapes[1:] + shapes[2:] * (CHUNKS - 1),
        [after(wavefield, data[0])],
        cost=LARGE,
    )
    waves = [[head, rest]] + [[w] for w in others]
    gathered = [[[swap("row", d, w) for w in ws] for d in range(1, rs)] for ws in waves]
    wholes = [whole, *others]

    second, basis = call(
        load_kernel,
        "load_factors",
        [((columns, 2 * rows, terms, tile), BF16), ((2, rows, columns, terms, tile), BF16)],
        [second_factor, basis_factor],
        in_specs=[HBM] * 2,
        scratch=[pltpu.SemaphoreType.DMA((2, 2 * rows))],
        cost=LARGE,
    )
    second = second.reshape(columns, 2 * rows * terms, tile)
    basis = basis.reshape(2, rows, columns * terms, tile)
    nears = call(
        near_kernel,
        "near_products",
        [((rows, columns * terms, width), F32)] * CHUNKS,
        [second, *[m for w in wholes for m in share([w])]],
        scratch=[pltpu.VMEM((columns, tile, width), BF16)],
        limit=16 * MIB,
        cost=1,
    )

    def forward(c, mine, heads):
        split = zs if c else SPLIT
        shape, piece = (zs, rows, span, width), (zs // split, rows, span, width)
        pieces = [m for slot in mine for m in slot]
        n = sum(m.shape[0] for m in mine[0])
        return call(
            functools.partial(forward_kernel, z_offsets, [len(slot) for slot in mine], len(heads)),
            "forward_product",
            [(shape, F32)] + [(piece, BF16)] * split,
            [tile_ranks, *pieces, second, basis, nears[c], *heads],
            in_specs=[SM] + [VM] * (len(pieces) + 3 + len(heads)),
            scratch=[
                pltpu.VMEM((n, tile, width), BF16),
                pltpu.VMEM((rows, n * terms, width), F32),
                pltpu.VMEM((rows, tile, width), F32),
            ],
            limit=16 * MIB,
            cost=LARGE if c else 1,
        )

    def backward(c, pieces, spots):
        whole, parts = (columns, width, quarter), 2
        piece = (columns // parts, width, quarter)
        back, *outs = call(
            functools.partial(adjoint_kernel, list(range(1, rs)), spots),
            "adjoint_product",
            [((columns, rows * terms, width), BF16)]
            + [(whole, F32)] * (rs - 1)
            + [(piece, BF16)] * ((rs - 1) * parts),
            [tile_ranks, *pieces, basis, second],
            in_specs=[SM] + [VM] * (len(pieces) + 2),
            scratch=[
                pltpu.VMEM((rows, tile, width), BF16),
                pltpu.VMEM((columns, rows * terms, width), F32),
            ],
            limit=16 * MIB,
            cost=1,
        )
        keeps, sends = outs[: rs - 1], outs[rs - 1 :]
        own = call(
            own_kernel, "own_quarter", [(whole, F32), (whole, BF16)], [back, second], limit=16 * MIB, cost=OWN
        )
        return [own[0], *keeps], [own[1:]] + [sends[d * parts : (d + 1) * parts] for d in range(rs - 1)]

    mirrored, residuals, sent, totals, joined = [], [], [], [], []

    def front(c):
        earlier = [(mirrored[-1][1],)] if c else [(second, *nears), (second, data[1])]
        far_pieces = [[after(m, *e) for m, e in zip(slot, earlier)] for slot in gathered[c]]
        mine = list(far_pieces)
        for d in range(1, helps):
            mine.extend([swap("help", d, m) for m in slot] for slot in far_pieces)
        heads = []
        if c:
            mine[0][0] = after(mine[0][0], mirrored[-1][1])
        else:
            pieces = [slot[0] for slot in mine]
            heads = call(
                functools.partial(head_kernel, [1] * len(pieces)),
                "first_coefficients",
                [((rows, first * terms, width), F32)],
                [tile_ranks, *pieces, second, nears[0]],
                in_specs=[SM] + [VM] * (len(pieces) + 2),
                scratch=[pltpu.VMEM((first, tile, width), BF16)],
                limit=16 * MIB,
                cost=HEAD,
            )
            mine = [slot[1:] or slot for slot in mine]
        keep, *sends = forward(c, mine, heads)
        others = [swap("help", 1, send) for send in sends]
        kernel, stay = mirror_kernel, []
        if len(near) == 1:
            kernel, n = stay_kernel, len(others) // 2
            shape = (keep.shape[0] // 2, rows, span, width)
            stay, others = others[:n], others[n:]
            send = call(sums_kernel, "halve", [(shape, BF16)], [keep, *others], cost=1)[0]
            others = [swap("col", near[0], send)]
        else:
            for d in near:
                shape = (keep.shape[0] // 2, rows, span, width)
                keep, send = call(halve_kernel, "halve", [(shape, F32), (shape, BF16)], [keep, *others], cost=1)
                others = [swap("col", d, send)]
        if c:
            residual_of(c - 1, send)
            keep = after(keep, *residuals[c - 1])
        shape = (2, rows, span, width)
        mirrored.append(
            call(kernel, "mirror", [(shape, F32), (shape, BF16)], [keep, *stay, *others])
        )

    def residual_of(c, *earlier):
        keep, send = mirrored[c]
        residuals.append(
            call(
                functools.partial(residual_kernel, c),
                "residual",
                [((2, rows, span, width), BF16)],
                [after(keep, *earlier), swap("col", far, send), *data],
                cost=LARGE,
            )
        )

    def rear(c):
        pieces, offsets = list(residuals[c]), [[0, far]]
        for d in reversed(near):
            pieces = pieces + [swap("col", d, m) for m in pieces]
            offsets = offsets + [[o ^ d for o in os] for os in offsets]
        last = c + 1 == CHUNKS
        earlier = sent if last else [mirrored[c + 1][1]]
        pieces[1:] = [after(m, *earlier) for m in pieces[1:]]
        passed = list(pieces)
        if not last:
            block = ((1, rows, span, width), BF16)
            for m in pieces[1:]:
                passed.extend(call(spread_kernel, "spread", [block] * 2, [m], cost=1))
            passed[1 : len(pieces)] = []
            passed_offsets = offsets[:1] + [[o] for os in offsets[1:] for o in os]
        else:
            passed_offsets = offsets
        pieces = pieces + [swap("help", d, m) for d in range(1, helps) for m in passed]
        spots = [(o, 0) for o in offsets] + [(o, e) for e in range(1, helps) for o in passed_offsets]
        if not last:
            pieces[0] = after(pieces[0], mirrored[c + 1][1])
        else:
            joined.extend(call(join_kernel, "join", [(observed.shape, BF16)], [r[0] for r in residuals]))
            pieces[0] = after(pieces[0], *joined)
        keeps, sends = backward(c, pieces, spots)
        if not last:
            residual_of(c + 1, sends[0][0])
            keeps = [keeps[0]] + [after(k, *residuals[c + 1]) for k in keeps[1:]]
        shape = (columns, width, quarter)
        shared = [
            call(
                share_kernel,
                "adjoint_share",
                [(shape, BF16)],
                [k, *[swap("help", 1, m) for m in s]],
            )[0]
            for k, s in zip(keeps[1:], sends[1:])
        ]
        if last:
            totals[-1][0] = after(totals[-1][0], *shared)
            mine, theirs, *others = totals[-1]
            mine = call(total_kernel, "total", [(shape, F32)], [mine, *others], cost=1)[0]
            totals[-1] = call(total_kernel, "total", [(shape, F32)], [mine, theirs], cost=LARGE)
        else:
            sent.extend(shared)
        totals.append(
            [keeps[0], swap("help", 1, after(sends[0][0], *shared))]
            + [swap("row", d + 1, m) for d, m in enumerate(shared)]
        )

    for c in range(CHUNKS):
        front(c)
    for c in range(CHUNKS):
        rear(c)

    adjoint = call(
        final_kernel,
        "adjoint_sum",
        [(wavefield.shape, BF16)],
        [*totals[0], *totals[1]],
        out_specs=[HBM],
        scratch=[pltpu.VMEM(wavefield.shape, BF16), pltpu.SemaphoreType.DMA((4,))],
    )[0]
    return joined[0], adjoint


def solution(mesh):
    return jax.shard_map(
        body,
        mesh=mesh,
        in_specs=(
            P("freq", "col", ("row", "help"), None),
            P("freq", "row", "col", "help", None),
            P("freq", "row", "col", "help", None),
            P(("freq", "row"), "col"),
            P("freq", "row", ("col", "help"), None),
            P(("freq", "row"), ("col", "help"), None),
        ),
        out_specs=(
            P("freq", "row", ("col", "help"), None),
            P("freq", "col", ("row", "help"), None),
        ),
        check_vma=False,
    )
```
